32 devices in a mesh: dp: 16 (over z, x, core), tensor: 2 (over y).
Axes of the slice: x: 2, y: 2, z: 4, core: 2. Of those that a mesh axis runs over, the one named last changes fastest.
Arguments:
- hidden: bfloat16 [8192, 14336], P('dp', 'tensor'), may hold values from -76 to 76
- base_weight: bfloat16 [14336, 4096], P('tensor', 'dp'), may hold values from -0.046875 to 0.046875
- adapter_in: bfloat16 [256, 14336], P(None, 'tensor'), may hold values from -0.046875 to 0.046875
- adapter_out: bfloat16 [256, 4096], P(None, 'tensor'), may hold values from -0.375 to 0.375
- cotangent: bfloat16 [8192, 4096], P('dp', 'tensor'), may hold values from -0.06591797 to 0.06591797
Outputs:
- output: bfloat16 [8192, 4096], P('dp', 'tensor')
- grad_in: float32 [256, 14336], P('dp', 'tensor')
- grad_out: float32 [256, 4096], P('dp', 'tensor')
The draws below stay inside these ranges and needn't reach their ends.
All inputs are finite; a program needn't handle non-finite values.
Results may differ from the reference program's by a relative error of at most 0.0031.
Values may be sent and summed in bfloat16 or wider, within the bound.
No kernel may reach another device: no remote copies, remote signals or barrier semaphores. Data moves between devices by JAX's collectives and lax.ppermute only.
A program may use at most 128 MiB of HBM per device.

```python
import math
import jax
import jax.numpy as jnp
from jax import lax

FF = 14336
DOUT = 4096
RANK = 256
TOKENS = 8192


def draw_hidden(key, part):
    keys = jax.random.split(key, 3)
    row_pos = jnp.arange(TOKENS, dtype=jnp.float32) / max(TOKENS - 1, 1)
    col_pos = jnp.arange(FF, dtype=jnp.float32) / max(FF - 1, 1)
    row_rand = jnp.exp(jax.random.uniform(keys[0], (TOKENS, 1), jnp.float32, math.log(0.3), math.log(1.5)))
    col_rand = jnp.exp(jax.random.uniform(keys[1], (1, FF), jnp.float32, math.log(0.7), math.log(1.4)))
    values = jax.random.truncated_normal(keys[2], -4.0, 4.0, (TOKENS, FF), jnp.float32)
    scaled = values * row_rand * col_rand * (1.0 + 2.0 * row_pos)[:, None] * (1.0 + 2.0 * col_pos)[None, :]
    return scaled.astype(jnp.bfloat16)


def level_of(rng, extent, shards, least, high):
    gain, own = 1.0, jax.random.fold_in(rng, 6)
    for dim, parts in shards:
        steps = jnp.exp(jax.random.uniform(jax.random.fold_in(own, dim), (parts,), jnp.float32, least / len(shards), high / len(shards)))
        gain = gain * jnp.repeat(steps, extent[dim] // parts).reshape([-1 if axis == dim else 1 for axis in range(len(extent))])
    return gain


def normal_values(key, extent, width, bound, pieces=(), kind=jnp.bfloat16):
    drawn = jax.random.normal(key, extent, jnp.float32) * width
    if len(pieces) > 0:
        drawn = level_of(key, extent, pieces, -0.22, 0.18) * drawn
    return jnp.clip(drawn, min=-bound, max=bound).astype(kind)


def setup_inputs(seed: int = 0) -> dict:
    splits = jax.random.split(jax.random.key(seed), 6)
    hidden = draw_hidden(jax.random.fold_in(splits[5], 71), 0)
    base_weight = normal_values(splits[1], (FF, DOUT), FF ** -0.5, 0.046875, ((0, 2), (1, 16)))
    adapter_in = normal_values(splits[2], (RANK, FF), FF ** -0.5, 0.046875, ((1, 2),))
    adapter_out = normal_values(splits[3], (RANK, DOUT), RANK ** -0.5, 0.375, ((1, 2),))
    cotangent = normal_values(splits[4], (TOKENS, DOUT), (1.0 / TOKENS ** 0.5), 0.06591797, ((0, 16), (1, 2)))
    return {"hidden": hidden, "base_weight": base_weight, "adapter_in": adapter_in, "adapter_out": adapter_out, "cotangent": cotangent}


adapter_scale = 4.0
exp_rate = 0.25
tiny_eps = 1e-06

def inverse_sinh(value):
    return jnp.log(value + jnp.sqrt(1.0 + value * value))

def reference(hidden, base_weight, adapter_in, adapter_out, cotangent):
    contract_last = (((1,), (1,)), ((), ()))
    contract_first = (((0,), (0,)), ((), ()))
    square_sum = lax.optimization_barrier(jnp.sum(jnp.square(hidden.astype(jnp.float32)), axis=1))
    level = jnp.sqrt(square_sum / FF + tiny_eps)
    radius = exp_rate * level
    lift_factor = jnp.sinh(radius) / radius
    lorentz_raw = lax.dot_general(hidden, adapter_in, contract_last, preferred_element_type=jnp.float32)
    lorentz = lift_factor[:, None] * lorentz_raw
    norm_value = jnp.sqrt(lax.optimization_barrier(jnp.sum(lorentz * lorentz, axis=1)) + tiny_eps)
    phi_value = inverse_sinh(norm_value) / norm_value
    tangent = (phi_value[:, None] * lorentz).astype(jnp.bfloat16)
    base_sum = jnp.dot(hidden, base_weight, preferred_element_type=jnp.float32)
    adapter_term = jnp.dot(tangent, adapter_out, preferred_element_type=jnp.float32)
    output = (base_sum + adapter_scale * adapter_term).astype(jnp.bfloat16)
    grad_out = adapter_scale * lax.dot_general(tangent, cotangent, contract_first, preferred_element_type=jnp.float32)
    tangent_grad = adapter_scale * lax.dot_general(cotangent, adapter_out, contract_last, preferred_element_type=jnp.float32)
    inner_value = lax.optimization_barrier(jnp.sum(lorentz * tangent_grad, axis=1))
    coefficient = (1.0 / jnp.sqrt(1.0 + norm_value * norm_value) - phi_value) / (norm_value * norm_value)
    lorentz_grad = phi_value[:, None] * tangent_grad + (coefficient * inner_value)[:, None] * lorentz
    raw_grad = (lift_factor[:, None] * lorentz_grad).astype(jnp.bfloat16)
    grad_in = lax.dot_general(raw_grad, hidden, contract_first, preferred_element_type=jnp.float32)
    return (output, grad_in, grad_out)
```

```python
import jax
import jax.numpy as jnp
from jax import lax
from jax.sharding import PartitionSpec as P

adapter_scale = 4.0
exp_rate = 0.25
tiny_eps = 1e-06


def inverse_sinh(value):
    return jnp.log(value + jnp.sqrt(1.0 + value * value))


def plain_shards(hidden, base_weight, adapter_in, adapter_out, cotangent):
    feature_count = hidden.shape[1] * lax.axis_size("tensor")
    contract_last = (((1,), (1,)), ((), ()))
    contract_first = (((0,), (0,)), ((), ()))
    square_part = jnp.sum(jnp.square(hidden.astype(jnp.float32)), axis=1)
    rank_part = lax.dot_general(
        hidden, adapter_in, contract_last, preferred_element_type=jnp.float32
    )
    square_sum, lorentz_raw = lax.psum((square_part, rank_part), "tensor")
    level = jnp.sqrt(square_sum / feature_count + tiny_eps)
    radius = exp_rate * level
    lift_factor = jnp.sinh(radius) / radius
    lorentz = lift_factor[:, None] * lorentz_raw
    norm_value = jnp.sqrt(jnp.sum(lorentz * lorentz, axis=1) + tiny_eps)
    phi_value = inverse_sinh(norm_value) / norm_value
    tangent = (phi_value[:, None] * lorentz).astype(jnp.bfloat16)
    partial_cols = jnp.dot(
        hidden,
        lax.all_gather(base_weight, "dp", axis=1, tiled=True),
        preferred_element_type=jnp.float32,
    )
    base_sum = lax.psum_scatter(partial_cols, "tensor", scatter_dimension=1, tiled=True)
    adapter_term = jnp.dot(tangent, adapter_out, preferred_element_type=jnp.float32)
    output = (base_sum + adapter_scale * adapter_term).astype(jnp.bfloat16)
    out_part = adapter_scale * lax.dot_general(
        tangent, cotangent, contract_first, preferred_element_type=jnp.float32
    )
    cotan_later = adapter_scale * lax.dot_general(
        cotangent, adapter_out, contract_last, preferred_element_type=jnp.float32
    )
    tangent_grad = lax.psum(cotan_later, "tensor")
    inner_value = jnp.sum(lorentz * tangent_grad, axis=1)
    coefficient = (1.0 / jnp.sqrt(1.0 + norm_value * norm_value) - phi_value) / (
        norm_value * norm_value
    )
    lorentz_grad = (
        phi_value[:, None] * tangent_grad + (coefficient * inner_value)[:, None] * lorentz
    )
    raw_grad = (lift_factor[:, None] * lorentz_grad).astype(jnp.bfloat16)
    in_part = lax.dot_general(raw_grad, hidden, contract_first, preferred_element_type=jnp.float32)
    grad_in, grad_out = (
        lax.psum_scatter(in_part, "dp", scatter_dimension=0, tiled=True),
        lax.psum_scatter(out_part, "dp", scatter_dimension=0, tiled=True),
    )
    return (output, grad_in, grad_out)


GROUP = 4
LINE = 4
QUARTERS = 4
AHEAD = 2
core_swap = [(d, d ^ 1) for d in range(LINE * GROUP)]
x_swap = [(d, d ^ 2) for d in range(LINE * GROUP)]
both_swap = [(d, d ^ 3) for d in range(LINE * GROUP)]
pair_swap = [(0, 1), (1, 0)]


def line_pairs(sources, step):
    return [(z * GROUP + r, (z + step) * GROUP + r) for z in sources for r in range(GROUP)]


def after(value, *others):
    return lax.optimization_barrier((value, *others))[0]


def pick(cases, default):
    out = default
    for condition, value in cases:
        out = jnp.where(condition, value, out)
    return out


def dot32(a, b):
    return jnp.dot(a, b, preferred_element_type=jnp.float32)


def weight_streams(base_weight, z, early):
    rows = base_weight.shape[0] // QUARTERS
    own = [base_weight[i * rows : (i + 1) * rows] for i in range(QUARTERS)]
    left, right = [], []
    for s in range(3 * QUARTERS):
        for got, sign, inner in ((left, -1, 1), (right, 1, 2)):
            sent = own[s] if s < QUARTERS else got[s - QUARTERS]
            if AHEAD <= s:
                other = got[s - AHEAD] if s < 2 * QUARTERS + AHEAD else own[s - 2 * QUARTERS]
                sent = jnp.where(jnp.logical_and(early, z == inner), other, sent)
            hop = s // QUARTERS
            sources = [q for q in range(LINE) if 0 <= q + sign < LINE and 0 <= q - sign * hop < LINE]
            got.append(lax.ppermute(sent, "dp", line_pairs(sources, sign)))
    return left, right


def group_sum(part, x, core):
    rows, width = part.shape
    view = part.reshape(LINE, 2, 2, rows // (4 * LINE), width)
    got = lax.ppermute(jnp.where(core == 0, view[:, :, 1], view[:, :, 0]), "dp", core_swap)
    mine = jnp.where(core == 0, view[:, :, 0], view[:, :, 1]) + got
    sent = jnp.where(x == 0, mine[:, 1], mine[:, 0]).astype(jnp.bfloat16)
    kept = jnp.where(x == 0, mine[:, 0], mine[:, 1])
    return kept, lax.ppermute(sent, "dp", x_swap)


def line_sum(mine, z, holds):
    got_left = got_right = None
    for k in range(1, LINE):
        send_left = lax.dynamic_index_in_dim(mine, jnp.maximum(z + k - LINE, 0), 0, False)
        send_right = lax.dynamic_index_in_dim(mine, jnp.minimum(z + LINE - k, LINE - 1), 0, False)
        if k > 1:
            send_left = send_left + after(got_left, *holds[k - 1])
            send_right = send_right + after(got_right, *holds[k - 1])
        got_left = lax.ppermute(send_left, "dp", line_pairs(range(LINE - k, LINE), -1))
        got_right = lax.ppermute(send_right, "dp", line_pairs(range(0, k), 1))
    own = lax.dynamic_index_in_dim(mine, z, 0, False)
    return own + after(got_left, *holds[LINE - 1]) + after(got_right, *holds[LINE - 1])


def fast_shards(hidden, base_weight, adapter_in, adapter_out, cotangent):
    feature_count = hidden.shape[1] * 2
    tokens, depth = hidden.shape
    columns = base_weight.shape[1]
    contract_last = (((1,), (1,)), ((), ()))
    contract_first = (((0,), (0,)), ((), ()))
    place = lax.axis_index("dp")
    z, member = place // GROUP, place % GROUP
    x, core = member // 2, member % 2
    y = lax.axis_index("tensor")
    outer = jnp.logical_or(z == 0, z == LINE - 1)
    low = z < 2
    early = (z // 2) == y
    late = jnp.logical_not(early)

    left, right = weight_streams(base_weight, z, early)

    half = tokens // 2
    other_x0 = lax.ppermute(hidden[:half], "dp", x_swap)
    other_core = lax.ppermute(hidden, "dp", core_swap)
    rank_part = lax.dot_general(
        hidden, adapter_in, contract_last, preferred_element_type=jnp.float32
    )
    square_part = jnp.sum(jnp.square(hidden.astype(jnp.float32)), axis=1)
    rank_other = lax.ppermute(rank_part, "tensor", pair_swap)
    square_other = lax.ppermute(square_part, "tensor", pair_swap)
    cotan_part = adapter_scale * lax.dot_general(
        cotangent, adapter_out, contract_last, preferred_element_type=jnp.float32
    )
    cotan_other = lax.ppermute(cotan_part, "tensor", pair_swap)

    level = jnp.sqrt((square_part + square_other) / feature_count + tiny_eps)
    radius = exp_rate * level
    lift_factor = jnp.sinh(radius) / radius
    lorentz = lift_factor[:, None] * (rank_part + rank_other)
    norm_value = jnp.sqrt(jnp.sum(lorentz * lorentz, axis=1) + tiny_eps)
    phi_value = inverse_sinh(norm_value) / norm_value
    tangent = (phi_value[:, None] * lorentz).astype(jnp.bfloat16)
    tangent_grad = cotan_part + cotan_other
    inner_value = jnp.sum(lorentz * tangent_grad, axis=1)
    coefficient = (1.0 / jnp.sqrt(1.0 + norm_value * norm_value) - phi_value) / (
        norm_value * norm_value
    )
    lorentz_grad = (
        phi_value[:, None] * tangent_grad + (coefficient * inner_value)[:, None] * lorentz
    )
    raw_grad = (lift_factor[:, None] * lorentz_grad).astype(jnp.bfloat16)
    out_part = adapter_scale * lax.dot_general(
        tangent, cotangent, contract_first, preferred_element_type=jnp.float32
    )
    in_part = lax.dot_general(raw_grad, hidden, contract_first, preferred_element_type=jnp.float32)
    tangents = [tangent] + [
        lax.ppermute(tangent, "dp", swap) for swap in (core_swap, x_swap, both_swap)
    ]
    in_kept, in_got = group_sum(in_part, x, core)
    out_kept, out_got = group_sum(out_part, x, core)

    other_x1 = lax.ppermute(after(hidden, other_x0, left[3], right[3])[half:], "dp", x_swap)
    far0 = lax.ppermute(after(other_x0, left[3], right[3]), "dp", core_swap)
    far1 = lax.ppermute(after(other_x1, left[8], right[8]), "dp", core_swap)

    holds = [None] + [(left[s], right[s]) for s in (7, 8, 9)]
    in_mine = in_kept + after(in_got, left[6], right[6]).astype(jnp.float32)
    out_mine = out_kept + after(out_got, left[6], right[6]).astype(jnp.float32)
    grad_in = line_sum(in_mine, z, holds)
    grad_out = line_sum(out_mine, z, holds)

    far = [jnp.where(low, a, b) for a, b in zip(left, right)]
    near = [jnp.where(low, b, a) for a, b in zip(left[:QUARTERS], right[:QUARTERS])]
    end_early = jnp.logical_and(outer, early)
    end_late = jnp.logical_and(outer, late)
    mid_late = jnp.logical_and(jnp.logical_not(outer), late)
    first = jnp.concatenate(
        [
            pick([(end_early, far[2 + q]), (mid_late, near[q])], far[q])
            for q in range(QUARTERS)
        ]
    )
    second = jnp.concatenate(
        [
            pick([(end_early, far[6 + q]), (mid_late, far[q])], far[4 + q])
            for q in range(QUARTERS)
        ]
    )
    third = [
        pick(
            [
                (end_early, far[q if q < AHEAD else 8 + q]),
                (end_late, far[8 + q]),
                (mid_late, far[4 + q]),
            ],
            near[q],
        )
        for q in range(QUARTERS)
    ]
    third_head, third_tail = jnp.concatenate(third[:3]), third[3]

    pieces = [[hidden], [other_core], [other_x0, other_x1], [far0, far1]]
    cut = third_head.shape[0]

    def products(block):
        return [jnp.concatenate([dot32(p, block) for p in ps]) for ps in pieces]

    sum_own = products(base_weight)
    sum_first = products(first)
    sum_second = products(second)
    sum_third = [
        jnp.concatenate(
            [dot32(p[:, :cut], third_head) + dot32(p[:, cut:], third_tail) for p in ps]
        )
        for ps in pieces
    ]
    flip = jnp.logical_and(late, jnp.logical_not(outer)).astype(jnp.int32)
    parity = (z % 2) ^ flip

    scale = jnp.float32(adapter_scale)
    output = jnp.zeros((tokens, adapter_out.shape[1]), jnp.bfloat16)
    swaps = (None, core_swap, x_swap, both_swap)
    for turn in range(2):
        offset = (parity ^ turn) * (GROUP * columns)
        factor = lax.dynamic_slice_in_dim(adapter_out, offset + member * columns, columns, 1)
        for m in (3, 2, 1, 0):
            if turn == 0:
                sent = jnp.where(early, sum_first[m], sum_own[m])
                kept = jnp.where(early, sum_own[m], sum_second[m])
            else:
                sent = jnp.where(early, sum_second[m], sum_first[m]).astype(jnp.bfloat16)
                kept = sum_third[m]
            total = kept + lax.ppermute(sent, "tensor", pair_swap).astype(jnp.float32)
            done = (total + scale * dot32(tangents[m], factor)).astype(jnp.bfloat16)
            if m:
                done = lax.ppermute(done, "dp", swaps[m])
            output = lax.dynamic_update_slice(
                output, done, (0, offset + (member ^ m) * columns)
            )
    return (output, grad_in, grad_out)


def solution(mesh):
    fits = mesh.shape["dp"] == LINE * GROUP and mesh.shape["tensor"] == 2
    return jax.shard_map(
        fast_shards if fits else plain_shards,
        mesh=mesh,
        in_specs=(
            P("dp", "tensor"),
            P("tensor", "dp"),
            P(None, "tensor"),
            P(None, "tensor"),
            P("dp", "tensor"),
        ),
        out_specs=(P("dp", "tensor"), P("dp", "tensor"), P("dp", "tensor")),
        check_vma=False,
    )
```

```python
import functools

import jax
import jax.numpy as jnp
from jax import lax
from jax.experimental import pallas as pl
from jax.experimental.pallas import tpu as pltpu
from jax.sharding import PartitionSpec as P

adapter_scale = 4.0
exp_rate = 0.25
tiny_eps = 1e-06


def inverse_sinh(value):
    return jnp.log(value + jnp.sqrt(1.0 + value * value))


def plain_shards(hidden, base_weight, adapter_in, adapter_out, cotangent):
    feature_count = hidden.shape[1] * lax.axis_size("tensor")
    contract_last = (((1,), (1,)), ((), ()))
    contract_first = (((0,), (0,)), ((), ()))
    square_part = jnp.sum(jnp.square(hidden.astype(jnp.float32)), axis=1)
    rank_part = lax.dot_general(
        hidden, adapter_in, contract_last, preferred_element_type=jnp.float32
    )
    square_sum, lorentz_raw = lax.psum((square_part, rank_part), "tensor")
    level = jnp.sqrt(square_sum / feature_count + tiny_eps)
    radius = exp_rate * level
    lift_factor = jnp.sinh(radius) / radius
    lorentz = lift_factor[:, None] * lorentz_raw
    norm_value = jnp.sqrt(jnp.sum(lorentz * lorentz, axis=1) + tiny_eps)
    phi_value = inverse_sinh(norm_value) / norm_value
    tangent = (phi_value[:, None] * lorentz).astype(jnp.bfloat16)
    partial_cols = jnp.dot(
        hidden,
        lax.all_gather(base_weight, "dp", axis=1, tiled=True),
        preferred_element_type=jnp.float32,
    )
    base_sum = lax.psum_scatter(partial_cols, "tensor", scatter_dimension=1, tiled=True)
    adapter_term = jnp.dot(tangent, adapter_out, preferred_element_type=jnp.float32)
    output = (base_sum + adapter_scale * adapter_term).astype(jnp.bfloat16)
    out_part = adapter_scale * lax.dot_general(
        tangent, cotangent, contract_first, preferred_element_type=jnp.float32
    )
    cotan_later = adapter_scale * lax.dot_general(
        cotangent, adapter_out, contract_last, preferred_element_type=jnp.float32
    )
    tangent_grad = lax.psum(cotan_later, "tensor")
    inner_value = jnp.sum(lorentz * tangent_grad, axis=1)
    coefficient = (1.0 / jnp.sqrt(1.0 + norm_value * norm_value) - phi_value) / (
        norm_value * norm_value
    )
    lorentz_grad = (
        phi_value[:, None] * tangent_grad + (coefficient * inner_value)[:, None] * lorentz
    )
    raw_grad = (lift_factor[:, None] * lorentz_grad).astype(jnp.bfloat16)
    in_part = lax.dot_general(raw_grad, hidden, contract_first, preferred_element_type=jnp.float32)
    grad_in, grad_out = (
        lax.psum_scatter(in_part, "dp", scatter_dimension=0, tiled=True),
        lax.psum_scatter(out_part, "dp", scatter_dimension=0, tiled=True),
    )
    return (output, grad_in, grad_out)


GROUP = 4
LINE = 4
HALVES = 2
core_swap = [(d, d ^ 1) for d in range(LINE * GROUP)]
x_swap = [(d, d ^ 2) for d in range(LINE * GROUP)]
both_swap = [(d, d ^ 3) for d in range(LINE * GROUP)]
pair_swap = [(0, 1), (1, 0)]


def line_pairs(sources, step):
    return [(z * GROUP + r, (z + step) * GROUP + r) for z in sources for r in range(GROUP)]


def pick(cases, default):
    out = default
    for condition, value in cases:
        out = jnp.where(condition, value, out)
    return out


def dot32(a, b):
    return jnp.dot(a, b, preferred_element_type=jnp.float32)


ROWS = 256
COST = 0.01


def product_kernel(plan, sources, blocks, has_base, *refs):
    code, refs = refs[0], refs[1:]
    weights, refs = refs[: sources[0]], refs[sources[0] :]
    hiddens, refs = refs[: sources[1]], refs[sources[1] :]
    (base, other, tangent, factor), refs = (refs[:4], refs[4:]) if has_base else ((None,) * 4, refs)
    out, weight, slots, weight_sem, slot_sems = refs
    first_column = plan[1]
    depth = weight.shape[0]
    step = depth // len(plan[0])

    def weight_copy(c, candidate):
        source, row = candidate
        return pltpu.make_async_copy(
            weights[source].at[pl.ds(row, step)],
            weight.at[pl.ds(c * step, step)],
            weight_sem.at[c],
        )

    def hidden_copies(b):
        copies, at = [], 0
        for source, row, rows in blocks[b]:
            copies.append(
                pltpu.make_async_copy(
                    hiddens[source].at[pl.ds(row, rows), pl.ds(first_column, depth)],
                    slots.at[b % 2, pl.ds(at, rows)],
                    slot_sems.at[b % 2],
                )
            )
            at += rows
        return copies

    for copy in hidden_copies(0):
        copy.start()
    for c, candidates in enumerate(plan[0]):
        if len(candidates) == 1:
            weight_copy(c, candidates[0]).start()
        for number, candidate in enumerate(candidates if len(candidates) > 1 else ()):

            @pl.when(code[c] == number)
            def _(c=c, candidate=candidate):
                weight_copy(c, candidate).start()

    for copy in hidden_copies(1):
        copy.start()
    for c, candidates in enumerate(plan[0]):
        weight_copy(c, candidates[0]).wait()

    def body(b, carry):
        slot = lax.rem(b, 2)
        for number in range(len(blocks)):

            @pl.when(b == number)
            def _(number=number):
                for copy in hidden_copies(number):
                    copy.wait()

        rows = pl.ds(pl.multiple_of(b * ROWS, ROWS), ROWS)
        total = jnp.dot(slots[slot], weight[...], preferred_element_type=jnp.float32)
        if base is not None:
            term = jnp.dot(tangent[rows, :], factor[...], preferred_element_type=jnp.float32)
            total = total + base[rows, :] + other[rows, :].astype(jnp.float32)
            total = total + jnp.float32(adapter_scale) * term
        out[rows, :] = total.astype(out.dtype)
        for number in range(2, len(blocks)):

            @pl.when(b + 2 == number)
            def _(number=number):
                for copy in hidden_copies(number):
                    copy.start()

        return carry

    lax.fori_loop(0, len(blocks), body, 0)


def product(code, step, chunks, hiddens, first_column=0, extra=(), dtype=jnp.float32):
    weights, candidates = [], []
    for chunk in chunks:
        for array, _ in chunk:
            if not any(array is weight for weight in weights):
                weights.append(array)
        candidates.append(
            tuple(
                ([array is weight for weight in weights].index(True), row) for array, row in chunk
            )
        )
    depth = step * len(chunks)
    columns = weights[0].shape[1]
    blocks, room = [], 0
    for number, array in enumerate(hiddens):
        row = 0
        while row < array.shape[0]:
            if room == 0:
                blocks.append([])
                room = ROWS
            rows = min(room, array.shape[0] - row)
            blocks[-1].append((number, row, rows))
            row, room = row + rows, room - rows
    height = len(blocks) * ROWS
    anywhere = pl.BlockSpec(memory_space=pl.ANY)
    whole = pl.BlockSpec(memory_space=pltpu.VMEM)
    operands = [code, *weights, *hiddens, *extra]
    in_specs = [pl.BlockSpec(memory_space=pltpu.SMEM)]
    in_specs += [anywhere] * (len(weights) + len(hiddens)) + [whole] * len(extra)
    kernel = functools.partial(
        product_kernel,
        (tuple(candidates), first_column),
        (len(weights), len(hiddens)),
        blocks,
        len(extra) > 0,
    )
    return pl.pallas_call(
        kernel,
        out_shape=jax.ShapeDtypeStruct((height, columns), dtype),
        in_specs=in_specs,
        out_specs=whole,
        scratch_shapes=[
            pltpu.VMEM((depth, columns), jnp.bfloat16),
            pltpu.VMEM((2, ROWS, depth), jnp.bfloat16),
            pltpu.SemaphoreType.DMA((len(chunks),)),
            pltpu.SemaphoreType.DMA((2,)),
        ],
        compiler_params=pltpu.CompilerParams(vmem_limit_bytes=32 * 2**20),
        cost_estimate=pl.CostEstimate(
            flops=int(2 * height * depth * columns * COST),
            bytes_accessed=int(2 * depth * (height + columns) * COST),
            transcendentals=0,
        ),
    )(*operands)


TILE = 1024
LANES = 128


def shared_kernel(in_steps, hidden, adapter_in, cotangent, adapter_out, out):
    number = pl.program_id(0)
    rank = adapter_in.shape[0]
    contract_last = (((1,), (1,)), ((), ()))

    @pl.when(number == 0)
    def _():
        out[...] = jnp.zeros_like(out)

    @pl.when(number < in_steps)
    def _():
        rows = hidden[...]
        out[:, :rank] += lax.dot_general(
            rows, adapter_in[...], contract_last, preferred_element_type=jnp.float32
        )
        wide = rows.astype(jnp.float32)
        squares = jnp.sum(wide * wide, axis=1, keepdims=True)
        out[:, 2 * rank :] += jnp.broadcast_to(squares, (rows.shape[0], LANES))

    @pl.when(number >= in_steps)
    def _():
        out[:, rank : 2 * rank] += adapter_scale * lax.dot_general(
            cotangent[...], adapter_out[...], contract_last, preferred_element_type=jnp.float32
        )


def shared_sums(hidden, adapter_in, cotangent, adapter_out):
    tokens, rank = hidden.shape[0], adapter_in.shape[0]
    in_steps, out_steps = hidden.shape[1] // TILE, cotangent.shape[1] // TILE
    early = lambda i: (0, jnp.minimum(i, in_steps - 1))
    late = lambda i: (0, jnp.maximum(i - in_steps, 0))
    return pl.pallas_call(
        functools.partial(shared_kernel, in_steps),
        grid=(in_steps + out_steps,),
        out_shape=jax.ShapeDtypeStruct((tokens, 2 * rank + LANES), jnp.float32),
        in_specs=[
            pl.BlockSpec((tokens, TILE), early),
            pl.BlockSpec((rank, TILE), early),
            pl.BlockSpec((tokens, TILE), late),
            pl.BlockSpec((rank, TILE), late),
        ],
        out_specs=pl.BlockSpec((tokens, 2 * rank + LANES), lambda i: (0, 0)),
        compiler_params=pltpu.CompilerParams(vmem_limit_bytes=32 * 2**20),
        cost_estimate=pl.CostEstimate(
            flops=int(2 * tokens * rank * TILE * (in_steps + out_steps) * COST),
            bytes_accessed=int(2 * TILE * (tokens + rank) * (in_steps + out_steps) * COST),
            transcendentals=0,
        ),
    )(hidden, adapter_in, cotangent, adapter_out)


def lift_of(radius):
    square = radius * radius
    series = 1.0 + square / 6.0 * (
        1.0 + square / 20.0 * (1.0 + square / 42.0 * (1.0 + square / 72.0))
    )
    large = (jnp.exp(radius) - jnp.exp(-radius)) * 0.5 / radius
    return jnp.where(radius < 1.0, series, large)


def gradient_kernel(
    in_steps, feature_count, own, other, order, hidden, cotangent, tangent_out, sent, kept, left_in, left_out
):
    number = pl.program_id(0)
    rank, half = order.shape[0], sent.shape[0]

    @pl.when(number == 0)
    def _():
        total = own[...] + other[...]
        raw, tangent_grad = total[:, :rank], total[:, rank : 2 * rank]
        square_sum = total[:, 2 * rank : 2 * rank + 1]
        level = jnp.sqrt(square_sum / feature_count + tiny_eps)
        lift_factor = lift_of(exp_rate * level)
        lorentz = lift_factor * raw
        norm_value = jnp.sqrt(jnp.sum(lorentz * lorentz, axis=1, keepdims=True) + tiny_eps)
        phi_value = inverse_sinh(norm_value) / norm_value
        tangent = (phi_value * lorentz).astype(jnp.bfloat16)
        inner_value = jnp.sum(lorentz * tangent_grad, axis=1, keepdims=True)
        coefficient = (1.0 / jnp.sqrt(1.0 + norm_value * norm_value) - phi_value) / (
            norm_value * norm_value
        )
        lorentz_grad = phi_value * tangent_grad + (coefficient * inner_value) * lorentz
        raw_grad = (lift_factor * lorentz_grad).astype(jnp.bfloat16)
        tangent_out[...] = tangent
        contract_last = (((1,), (1,)), ((), ()))
        for target, value in ((left_in, raw_grad), (left_out, tangent)):
            target[...] = lax.dot_general(
                order[...], value, contract_last, preferred_element_type=jnp.float32
            ).astype(jnp.bfloat16)

    @pl.when(number < in_steps)
    def _():
        total = jnp.dot(left_in[...], hidden[...], preferred_element_type=jnp.float32)
        sent[...] = total[:half]
        kept[...] = total[half:]

    @pl.when(number >= in_steps)
    def _():
        total = adapter_scale * jnp.dot(
            left_out[...], cotangent[...], preferred_element_type=jnp.float32
        )
        sent[...] = total[:half]
        kept[...] = total[half:]


def gradients(own, other, order, feature_count, hidden, cotangent):
    rank, tokens = order.shape[0], hidden.shape[0]
    in_steps, out_steps = hidden.shape[1] // TILE, cotangent.shape[1] // TILE
    steps = in_steps + out_steps
    shape = jax.ShapeDtypeStruct((rank // 2, steps * TILE), jnp.float32)
    part = pl.BlockSpec((rank // 2, TILE), lambda i: (0, i))
    return pl.pallas_call(
        functools.partial(gradient_kernel, in_steps, feature_count),
        grid=(steps,),
        out_shape=(jax.ShapeDtypeStruct((tokens, rank), jnp.bfloat16), shape, shape),
        in_specs=[
            pl.BlockSpec(own.shape, lambda i: (0, 0)),
            pl.BlockSpec(own.shape, lambda i: (0, 0)),
            pl.BlockSpec(order.shape, lambda i: (0, 0)),
            pl.BlockSpec((tokens, TILE), lambda i: (0, jnp.minimum(i, in_steps - 1))),
            pl.BlockSpec((tokens, TILE), lambda i: (0, jnp.maximum(i - in_steps, 0))),
        ],
        out_specs=(pl.BlockSpec((tokens, rank), lambda i: (0, 0)), part, part),
        scratch_shapes=[pltpu.VMEM((rank, tokens), jnp.bfloat16)] * 2,
        compiler_params=pltpu.CompilerParams(vmem_limit_bytes=32 * 2**20),
        cost_estimate=pl.CostEstimate(
            flops=int(2 * rank * tokens * steps * TILE * COST),
            bytes_accessed=int((2 * tokens + 4 * rank) * steps * TILE * COST),
            transcendentals=0,
        ),
    )(own, other, order, hidden, cotangent)


def assemble_kernel(code, *refs):
    out = refs[-1]
    for number, piece in enumerate(refs[:-1]):

        @pl.when(pl.program_id(0) == number)
        def _(piece=piece):
            out[...] = piece[...]


def assemble(places, pieces):
    tokens, columns = pieces[0].shape
    return pl.pallas_call(
        assemble_kernel,
        grid_spec=pltpu.PrefetchScalarGridSpec(
            num_scalar_prefetch=1,
            grid=(len(pieces),),
            in_specs=[pl.BlockSpec((tokens, columns), lambda i, code: (0, 0))] * len(pieces),
            out_specs=pl.BlockSpec((tokens, columns), lambda i, code: (0, code[i])),
        ),
        out_shape=jax.ShapeDtypeStruct((tokens, columns * len(pieces)), pieces[0].dtype),
        compiler_params=pltpu.CompilerParams(vmem_limit_bytes=32 * 2**20),
    )(jnp.stack(places).astype(jnp.int32), *pieces)


class Held(dict):
    def gate(self, *names):
        names = list(dict.fromkeys(names))
        for name, value in zip(names, lax.optimization_barrier(tuple(self[n] for n in names))):
            self[name] = value

    def all(self, letter, numbers):
        return [self[letter, i] for i in numbers]


def fast_shards(hidden, base_weight, adapter_in, adapter_out, cotangent):
    feature_count = hidden.shape[1] * 2
    tokens, depth = hidden.shape
    columns = base_weight.shape[1]
    place = lax.axis_index("dp")
    z, member = place // GROUP, place % GROUP
    x, core = member // 2, member % 2
    y = lax.axis_index("tensor")
    outer = jnp.logical_or(z == 0, z == LINE - 1)
    inner = jnp.logical_not(outer)
    early = (z // 2) == y
    late = jnp.logical_not(early)
    side = jnp.where(z < 2, 0, 1)
    scale = jnp.float32(adapter_scale)
    parts, slots = 4, 3 * HALVES
    rows, step = depth // HALVES, tokens // parts
    held = Held()
    held["own", 0], held["x", 0] = base_weight[:rows], hidden[:step]
    held["weight"], held["hidden"] = base_weight, hidden

    def send_weight(s):
        hop = s // HALVES
        if hop == LINE - 2:
            far = [jnp.where(side == 0, held["left", q], held["right", q]) for q in (2, 3)]
            far.append(held["own", 1])
            sent = jnp.where(jnp.logical_and(early, inner), far[s - 3], far[s - 4])
            pairs = line_pairs([1], -1) + line_pairs([LINE - 2], 1)
            held["left", s] = held["right", s] = lax.ppermute(sent, "dp", pairs)
            return
        for name, sign, last in (("left", -1, 1), ("right", 1, LINE - 2)):
            sent = held["own", s] if s < HALVES else held[name, s - HALVES]
            if s > 0:
                other = held[name, s - 1]
                sent = jnp.where(jnp.logical_and(early, z == last), other, sent)
            sources = [q for q in range(LINE) if 0 <= q + sign < LINE and 0 <= q - sign * hop < LINE]
            held[name, s] = lax.ppermute(sent, "dp", line_pairs(sources, sign))

    def send_hidden(i):
        if i:
            held["x", i] = held["hidden"][i * step : (i + 1) * step]
        held["x", i] = lax.ppermute(held["x", i], "dp", x_swap)

    def over_core(name, result=None):
        held[result or name] = lax.ppermute(held[name], "dp", core_swap)

    def pass_hidden(i):
        over_core(("x", i), ("far", i))

    def send_sums(k):
        sent = lax.dynamic_index_in_dim(held["mine"], z ^ k, 0, False).astype(jnp.bfloat16)
        pairs = [(q * GROUP + r, (q ^ k) * GROUP + r) for q in range(LINE) for r in range(GROUP)]
        held["got", k] = lax.ppermute(sent, "dp", pairs)

    def codes(default, *cases):
        return pick(cases, default).astype(jnp.int32)[None]

    def streams(*numbers):
        return [(held[name, s], 0) for s in numbers for name in ("left", "right")]

    def window(s, *names):
        names = [("left", s), ("right", s), "weight", *names]
        held.gate(*names)
        held["own", 1] = held["weight"][rows:]
        if s < LINE - 1:
            send_weight(s + 1)
        if s == LINE - 1:
            send_weight(s + 1)
            send_weight(s + 2)

    end_early = jnp.logical_and(outer, early)
    end_late = jnp.logical_and(outer, late)
    inner_late = jnp.logical_and(inner, late)
    none = jnp.zeros((1,), jnp.int32)
    first_code = codes(2 + side, (end_early, side), (inner_late, 3 - side))
    first_code = jnp.concatenate([first_code] * HALVES)
    second_code = codes(4 + side, (end_early, side), (inner_late, 2 + side))
    second_code = jnp.concatenate([second_code] * HALVES)
    third_code = [
        codes(
            1 - side,
            (end_early, side + (0 if q == 0 else 2)),
            (end_late, 2 + side),
            (inner_late, 4 + side),
        )
        for q in range(HALVES)
    ]

    send_weight(0)
    send_hidden(0)
    held["core"] = lax.ppermute(hidden, "dp", core_swap)
    held["shared"] = shared_sums(hidden, adapter_in, cotangent, adapter_out)
    held["shared other"] = lax.ppermute(held["shared"], "tensor", pair_swap)
    rank = adapter_in.shape[0]
    share = rank // (LINE * GROUP)
    row = jnp.arange(rank)
    which = row // (LINE * share)
    owner = member ^ jnp.where(which == 0, 3, jnp.where(which == 1, 1, jnp.where(which == 2, 2, 0)))
    column = (row // share % LINE) * (GROUP * share) + owner * share + row % share
    held["order"] = (column[:, None] == jnp.arange(rank)[None, :]).astype(jnp.bfloat16)

    window(0, ("x", 0), "hidden")
    send_hidden(1)
    held["t", 0], held["sent"], held["kept"] = gradients(
        held["shared"], held["shared other"], held["order"], feature_count, hidden, cotangent
    )
    over_core("sent")

    window(1, ("x", 1), "hidden", "core", "kept", ("t", 0))
    send_hidden(2)
    pass_hidden(0)
    near = [hidden, held["core"]]
    whole_weight = [[(base_weight, 0)]]
    held["own sum", 0] = product(none, depth, whole_weight, near)

    window(2, ("x", 2), "hidden", ("far", 0), "sent", "kept", ("own sum", 0))
    send_hidden(3)
    pass_hidden(1)
    pass_hidden(2)
    sums = held["kept"] + held["sent"]
    flat = sums[: rank // 4].astype(jnp.bfloat16)
    held["sent"] = jnp.concatenate([flat, held["t", 0].reshape(flat.shape[0], -1)], axis=1)
    held["kept"] = sums[rank // 4 :]
    first = [streams(1 + q, q) for q in range(HALVES)]
    held["first sum", 0] = product(first_code, rows, first, near)

    held["y", 0] = jnp.where(early, held["first sum", 0], held["own sum", 0])

    window(3, ("x", 3), ("far", 1), ("far", 2), "sent", "kept", ("first sum", 0), ("y", 0))
    pass_hidden(3)
    held["sent"] = lax.ppermute(held["sent"], "dp", x_swap)
    held["y", 0] = lax.ppermute(held["y", 0], "tensor", pair_swap)
    half = parts // 2
    for h in (1, 2):
        pieces = range((h - 1) * half, h * half)
        members = held.all("x", pieces) + held.all("far", pieces)
        held["own sum", h] = product(none, depth, whole_weight, members)
        held["first sum", h] = product(first_code, rows, first, members)

    def in_order(name):
        a, b = held[name, 1], held[name, 2]
        cut = a.shape[0] // 2
        return jnp.concatenate([a[:cut], b[:cut], a[cut:], b[cut:]])

    first_sums = [held["first sum", 0], in_order("first sum")]
    own_sums = [held["own sum", 0], in_order("own sum")]
    held["y", 1] = lax.ppermute(
        jnp.where(early, first_sums[1], own_sums[1]), "tensor", pair_swap
    )

    window(4, "sent", "kept", *[("far", i) for i in range(parts)], ("y", 0), ("y", 1), ("t", 0))
    width = held["kept"].shape[1]
    held["t", 2] = held["sent"][:, width:].reshape(tokens, -1)
    for m in (0, 2):
        held["t", m + 1] = held["t", m]
        over_core(("t", m + 1))
    held["mine"] = held["kept"] + held["sent"][:, :width].astype(jnp.float32)
    held["mine"] = held["mine"].reshape(LINE, share, -1)
    for k in (1, 2, 3):
        send_sums(k)
    far = held.all("x", range(parts)) + held.all("far", range(parts))
    groups = (near, far)
    second = [streams(3 + q, q, 2 + q) for q in range(HALVES)]
    third = [streams(q, 4 + q, 2 + q) for q in range(HALVES)]
    for h in (1, 0):
        held["second sum", h] = product(second_code, rows, second, groups[h])
        sent = jnp.where(early, held["second sum", h], first_sums[h])
        held["w", h] = lax.ppermute(sent.astype(jnp.bfloat16), "tensor", pair_swap)
    parity = (z % 2) ^ inner_late.astype(jnp.int32)
    blocks = [(parity ^ turn) * GROUP for turn in range(2)]
    factors = [
        lax.dynamic_slice_in_dim(adapter_out, (block + member) * columns, columns, 1)
        for block in blocks
    ]
    swaps = (None, core_swap, x_swap, both_swap)
    numbers = ((0, 1), (2, 3))
    places, pieces = [], []

    def give_out(turn, h, value):
        for i, m in reversed(list(enumerate(numbers[h]))):
            piece = value[i * tokens : (i + 1) * tokens]
            if m:
                piece = lax.ppermute(piece, "dp", swaps[m])
            places.append(blocks[turn] + (member ^ m))
            pieces.append(piece)

    for h in (1, 0):
        held["third sum", h] = product(third_code[0], rows, third[:1], groups[h])
    group_tangents = [jnp.concatenate(held.all("t", numbers[h])) for h in range(2)]
    for h in (1, 0):
        total = jnp.where(early, own_sums[h], held["second sum", h]) + held["y", h]
        total = total + scale * dot32(group_tangents[h], factors[0])
        give_out(0, h, total.astype(jnp.bfloat16))

    window(5, ("third sum", 0), ("third sum", 1))
    for h in (1, 0):
        chunk = [streams(1, 5, 3)]
        extra = (held["third sum", h], held["w", h], group_tangents[h], factors[1])
        value = product(third_code[1], rows, chunk, groups[h], rows, extra, jnp.bfloat16)
        give_out(1, h, value)
    output = assemble(places, pieces)
    grads = lax.dynamic_index_in_dim(held["mine"], z, 0, False)
    held["grads"] = sum((held["got", k].astype(jnp.float32) for k in (1, 2, 3)), grads)
    return (output, held["grads"][:, :depth], held["grads"][:, depth:])


def solution(mesh):
    fits = mesh.shape["dp"] == LINE * GROUP and mesh.shape["tensor"] == 2
    return jax.shard_map(
        fast_shards if fits else plain_shards,
        mesh=mesh,
        in_specs=(
            P("dp", "tensor"),
            P("tensor", "dp"),
            P(None, "tensor"),
            P(None, "tensor"),
            P("dp", "tensor"),
        ),
        out_specs=(P("dp", "tensor"), P("dp", "tensor"), P("dp", "tensor")),
        check_vma=False,
    )
```

```python
import functools

import jax
import jax.numpy as jnp
from jax import lax
from jax.experimental import pallas as pl
from jax.experimental.pallas import tpu as pltpu
from jax.sharding import PartitionSpec as P

adapter_scale = 4.0
exp_rate = 0.25
tiny_eps = 1e-06


def inverse_sinh(value):
    return jnp.log(value + jnp.sqrt(1.0 + value * value))


def plain_shards(hidden, base_weight, adapter_in, adapter_out, cotangent):
    feature_count = hidden.shape[1] * lax.axis_size("tensor")
    contract_last = (((1,), (1,)), ((), ()))
    contract_first = (((0,), (0,)), ((), ()))
    square_part = jnp.sum(jnp.square(hidden.astype(jnp.float32)), axis=1)
    rank_part = lax.dot_general(
        hidden, adapter_in, contract_last, preferred_element_type=jnp.float32
    )
    square_sum, lorentz_raw = lax.psum((square_part, rank_part), "tensor")
    level = jnp.sqrt(square_sum / feature_count + tiny_eps)
    radius = exp_rate * level
    lift_factor = jnp.sinh(radius) / radius
    lorentz = lift_factor[:, None] * lorentz_raw
    norm_value = jnp.sqrt(jnp.sum(lorentz * lorentz, axis=1) + tiny_eps)
    phi_value = inverse_sinh(norm_value) / norm_value
    tangent = (phi_value[:, None] * lorentz).astype(jnp.bfloat16)
    partial_cols = jnp.dot(
        hidden,
        lax.all_gather(base_weight, "dp", axis=1, tiled=True),
        preferred_element_type=jnp.float32,
    )
    base_sum = lax.psum_scatter(partial_cols, "tensor", scatter_dimension=1, tiled=True)
    adapter_term = jnp.dot(tangent, adapter_out, preferred_element_type=jnp.float32)
    output = (base_sum + adapter_scale * adapter_term).astype(jnp.bfloat16)
    out_part = adapter_scale * lax.dot_general(
        tangent, cotangent, contract_first, preferred_element_type=jnp.float32
    )
    cotan_later = adapter_scale * lax.dot_general(
        cotangent, adapter_out, contract_last, preferred_element_type=jnp.float32
    )
    tangent_grad = lax.psum(cotan_later, "tensor")
    inner_value = jnp.sum(lorentz * tangent_grad, axis=1)
    coefficient = (1.0 / jnp.sqrt(1.0 + norm_value * norm_value) - phi_value) / (
        norm_value * norm_value
    )
    lorentz_grad = (
        phi_value[:, None] * tangent_grad + (coefficient * inner_value)[:, None] * lorentz
    )
    raw_grad = (lift_factor[:, None] * lorentz_grad).astype(jnp.bfloat16)
    in_part = lax.dot_general(raw_grad, hidden, contract_first, preferred_element_type=jnp.float32)
    grad_in, grad_out = (
        lax.psum_scatter(in_part, "dp", scatter_dimension=0, tiled=True),
        lax.psum_scatter(out_part, "dp", scatter_dimension=0, tiled=True),
    )
    return (output, grad_in, grad_out)


GROUP = 4
LINE = 4
HALVES = 2
core_swap = [(d, d ^ 1) for d in range(LINE * GROUP)]
x_swap = [(d, d ^ 2) for d in range(LINE * GROUP)]
both_swap = [(d, d ^ 3) for d in range(LINE * GROUP)]
pair_swap = [(0, 1), (1, 0)]


def line_pairs(sources, step):
    return [(z * GROUP + r, (z + step) * GROUP + r) for z in sources for r in range(GROUP)]


def pick(cases, default):
    out = default
    for condition, value in cases:
        out = jnp.where(condition, value, out)
    return out


def dot32(a, b):
    return jnp.dot(a, b, preferred_element_type=jnp.float32)


ROWS = 256
COST = 0.01


def product_kernel(plan, sources, blocks, has_base, *refs):
    code, refs = refs[0], refs[1:]
    weights, refs = refs[: sources[0]], refs[sources[0] :]
    hiddens, refs = refs[: sources[1]], refs[sources[1] :]
    extra, refs = refs[:has_base], refs[has_base:]
    outs, (weight, slots, weight_sem, slot_sems) = refs[:-4], refs[-4:]
    out = outs[0]
    first_column = plan[1]
    depth = weight.shape[0]
    step = depth // len(plan[0])

    def weight_copy(c, candidate):
        source, row = candidate
        return pltpu.make_async_copy(
            weights[source].at[pl.ds(row, step)],
            weight.at[pl.ds(c * step, step)],
            weight_sem.at[c],
        )

    def hidden_copies(b):
        copies, at = [], 0
        for source, row, rows in blocks[b]:
            copies.append(
                pltpu.make_async_copy(
                    hiddens[source].at[pl.ds(row, rows), pl.ds(first_column, depth)],
                    slots.at[b % 2, pl.ds(at, rows)],
                    slot_sems.at[b % 2],
                )
            )
            at += rows
        return copies

    for copy in hidden_copies(0):
        copy.start()
    for c, candidates in enumerate(plan[0]):
        if len(candidates) == 1:
            weight_copy(c, candidates[0]).start()
        for number, candidate in enumerate(candidates if len(candidates) > 1 else ()):

            @pl.when(code[c] == number)
            def _(c=c, candidate=candidate):
                weight_copy(c, candidate).start()

    for copy in hidden_copies(1):
        copy.start()
    for c, candidates in enumerate(plan[0]):
        weight_copy(c, candidates[0]).wait()

    def body(b, carry):
        slot = lax.rem(b, 2)
        for number in range(len(blocks)):

            @pl.when(b == number)
            def _(number=number):
                for copy in hidden_copies(number):
                    copy.wait()

        rows = pl.ds(pl.multiple_of(b * ROWS, ROWS), ROWS)
        if len(extra) == 6:
            third = jnp.dot(
                slots[slot, :, :step], weight[:step], preferred_element_type=jnp.float32
            )
            outs[2][rows, :] = third
            total = extra[0][rows, :] + jnp.dot(
                slots[slot, :, step:], weight[step:], preferred_element_type=jnp.float32
            )
        else:
            total = jnp.dot(slots[slot], weight[...], preferred_element_type=jnp.float32)
        if len(extra) > 0:
            other, tangent, factor = extra[-3:]
            term = jnp.dot(tangent[rows, :], factor[...], preferred_element_type=jnp.float32)
            term = other[rows, :].astype(jnp.float32) + jnp.float32(adapter_scale) * term
        if len(extra) == 6:
            gives = code[len(plan[0])] == 1
            first, own = extra[1][rows, :], extra[2][rows, :]
            outs[1][rows, :] = (jnp.where(gives, own, total) + term).astype(outs[1].dtype)
            total = jnp.where(gives, total, first)
        elif len(extra) == 4:
            total = total + extra[0][rows, :] + term
        out[rows, :] = total.astype(out.dtype)
        for number in range(2, len(blocks)):

            @pl.when(b + 2 == number)
            def _(number=number):
                for copy in hidden_copies(number):
                    copy.start()

        return carry

    lax.fori_loop(0, len(blocks), body, 0)


def product(code, step, chunks, hiddens, first_column=0, extra=(), dtype=jnp.float32):
    weights, candidates = [], []
    for chunk in chunks:
        for array, _ in chunk:
            if not any(array is weight for weight in weights):
                weights.append(array)
        candidates.append(
            tuple(
                ([array is weight for weight in weights].index(True), row) for array, row in chunk
            )
        )
    depth = step * len(chunks)
    columns = weights[0].shape[1]
    blocks, room = [], 0
    for number, array in enumerate(hiddens):
        row = 0
        while row < array.shape[0]:
            if room == 0:
                blocks.append([])
                room = ROWS
            rows = min(room, array.shape[0] - row)
            blocks[-1].append((number, row, rows))
            row, room = row + rows, room - rows
    height = len(blocks) * ROWS
    anywhere = pl.BlockSpec(memory_space=pl.ANY)
    whole = pl.BlockSpec(memory_space=pltpu.VMEM)
    operands = [code, *weights, *hiddens, *extra]
    in_specs = [pl.BlockSpec(memory_space=pltpu.SMEM)]
    in_specs += [anywhere] * (len(weights) + len(hiddens)) + [whole] * len(extra)
    kernel = functools.partial(
        product_kernel,
        (tuple(candidates), first_column),
        (len(weights), len(hiddens)),
        blocks,
        len(extra),
    )
    shape = jax.ShapeDtypeStruct((height, columns), dtype)
    shapes = (shape, shape, jax.ShapeDtypeStruct((height, columns), jnp.float32))
    several = len(extra) == 6
    return pl.pallas_call(
        kernel,
        out_shape=shapes if several else shape,
        in_specs=in_specs,
        out_specs=(whole,) * 3 if several else whole,
        scratch_shapes=[
            pltpu.VMEM((depth, columns), jnp.bfloat16),
            pltpu.VMEM((2, ROWS, depth), jnp.bfloat16),
            pltpu.SemaphoreType.DMA((len(chunks),)),
            pltpu.SemaphoreType.DMA((2,)),
        ],
        compiler_params=pltpu.CompilerParams(vmem_limit_bytes=40 * 2**20),
        cost_estimate=pl.CostEstimate(
            flops=int(2 * height * depth * columns * COST),
            bytes_accessed=int(2 * depth * (height + columns) * COST),
            transcendentals=0,
        ),
    )(*operands)


TILE = 1024
LANES = 128


def shared_kernel(in_steps, hidden, adapter_in, cotangent, adapter_out, out):
    number = pl.program_id(0)
    rank = adapter_in.shape[0]
    contract_last = (((1,), (1,)), ((), ()))

    @pl.when(number == 0)
    def _():
        out[...] = jnp.zeros_like(out)

    @pl.when(number < in_steps)
    def _():
        rows = hidden[...]
        out[:, :rank] += lax.dot_general(
            rows, adapter_in[...], contract_last, preferred_element_type=jnp.float32
        )
        wide = rows.astype(jnp.float32)
        squares = jnp.sum(wide * wide, axis=1, keepdims=True)
        out[:, 2 * rank :] += jnp.broadcast_to(squares, (rows.shape[0], LANES))

    @pl.when(number >= in_steps)
    def _():
        out[:, rank : 2 * rank] += adapter_scale * lax.dot_general(
            cotangent[...], adapter_out[...], contract_last, preferred_element_type=jnp.float32
        )


def shared_sums(hidden, adapter_in, cotangent, adapter_out):
    tokens, rank = hidden.shape[0], adapter_in.shape[0]
    in_steps, out_steps = hidden.shape[1] // TILE, cotangent.shape[1] // TILE
    early = lambda i: (0, jnp.minimum(i, in_steps - 1))
    late = lambda i: (0, jnp.maximum(i - in_steps, 0))
    return pl.pallas_call(
        functools.partial(shared_kernel, in_steps),
        grid=(in_steps + out_steps,),
        out_shape=jax.ShapeDtypeStruct((tokens, 2 * rank + LANES), jnp.float32),
        in_specs=[
            pl.BlockSpec((tokens, TILE), early),
            pl.BlockSpec((rank, TILE), early),
            pl.BlockSpec((tokens, TILE), late),
            pl.BlockSpec((rank, TILE), late),
        ],
        out_specs=pl.BlockSpec((tokens, 2 * rank + LANES), lambda i: (0, 0)),
        compiler_params=pltpu.CompilerParams(vmem_limit_bytes=32 * 2**20),
        cost_estimate=pl.CostEstimate(
            flops=int(2 * tokens * rank * TILE * (in_steps + out_steps) * COST),
            bytes_accessed=int(2 * TILE * (tokens + rank) * (in_steps + out_steps) * COST),
            transcendentals=0,
        ),
    )(hidden, adapter_in, cotangent, adapter_out)


def lift_of(radius):
    square = radius * radius
    series = 1.0 + square / 6.0 * (
        1.0 + square / 20.0 * (1.0 + square / 42.0 * (1.0 + square / 72.0))
    )
    large = (jnp.exp(radius) - jnp.exp(-radius)) * 0.5 / radius
    return jnp.where(radius < 1.0, series, large)


def gradient_kernel(
    in_steps, feature_count, own, other, order, hidden, cotangent, tangent_out, sent, kept, left_in, left_out
):
    number = pl.program_id(0)
    rank, half = order.shape[0], sent.shape[0]

    @pl.when(number == 0)
    def _():
        total = own[...] + other[...]
        raw, tangent_grad = total[:, :rank], total[:, rank : 2 * rank]
        square_sum = total[:, 2 * rank : 2 * rank + 1]
        level = jnp.sqrt(square_sum / feature_count + tiny_eps)
        lift_factor = lift_of(exp_rate * level)
        lorentz = lift_factor * raw
        norm_value = jnp.sqrt(jnp.sum(lorentz * lorentz, axis=1, keepdims=True) + tiny_eps)
        phi_value = inverse_sinh(norm_value) / norm_value
        tangent = (phi_value * lorentz).astype(jnp.bfloat16)
        inner_value = jnp.sum(lorentz * tangent_grad, axis=1, keepdims=True)
        coefficient = (1.0 / jnp.sqrt(1.0 + norm_value * norm_value) - phi_value) / (
            norm_value * norm_value
        )
        lorentz_grad = phi_value * tangent_grad + (coefficient * inner_value) * lorentz
        raw_grad = (lift_factor * lorentz_grad).astype(jnp.bfloat16)
        tangent_out[...] = tangent
        contract_last = (((1,), (1,)), ((), ()))
        for target, value in ((left_in, raw_grad), (left_out, tangent)):
            target[...] = lax.dot_general(
                order[...], value, contract_last, preferred_element_type=jnp.float32
            ).astype(jnp.bfloat16)

    @pl.when(number < in_steps)
    def _():
        total = jnp.dot(left_in[...], hidden[...], preferred_element_type=jnp.float32)
        sent[...] = total[:half]
        kept[...] = total[half:]

    @pl.when(number >= in_steps)
    def _():
        total = adapter_scale * jnp.dot(
            left_out[...], cotangent[...], preferred_element_type=jnp.float32
        )
        sent[...] = total[:half]
        kept[...] = total[half:]


def gradients(own, other, order, feature_count, hidden, cotangent):
    rank, tokens = order.shape[0], hidden.shape[0]
    in_steps, out_steps = hidden.shape[1] // TILE, cotangent.shape[1] // TILE
    steps = in_steps + out_steps
    shape = jax.ShapeDtypeStruct((rank // 2, steps * TILE), jnp.float32)
    part = pl.BlockSpec((rank // 2, TILE), lambda i: (0, i))
    return pl.pallas_call(
        functools.partial(gradient_kernel, in_steps, feature_count),
        grid=(steps,),
        out_shape=(jax.ShapeDtypeStruct((tokens, rank), jnp.bfloat16), shape, shape),
        in_specs=[
            pl.BlockSpec(own.shape, lambda i: (0, 0)),
            pl.BlockSpec(own.shape, lambda i: (0, 0)),
            pl.BlockSpec(order.shape, lambda i: (0, 0)),
            pl.BlockSpec((tokens, TILE), lambda i: (0, jnp.minimum(i, in_steps - 1))),
            pl.BlockSpec((tokens, TILE), lambda i: (0, jnp.maximum(i - in_steps, 0))),
        ],
        out_specs=(pl.BlockSpec((tokens, rank), lambda i: (0, 0)), part, part),
        scratch_shapes=[pltpu.VMEM((rank, tokens), jnp.bfloat16)] * 2,
        compiler_params=pltpu.CompilerParams(vmem_limit_bytes=32 * 2**20),
        cost_estimate=pl.CostEstimate(
            flops=int(2 * rank * tokens * steps * TILE * COST),
            bytes_accessed=int((2 * tokens + 4 * rank) * steps * TILE * COST),
            transcendentals=0,
        ),
    )(own, other, order, hidden, cotangent)


def assemble_kernel(code, *refs):
    out = refs[-1]
    for number, piece in enumerate(refs[:-1]):

        @pl.when(pl.program_id(0) == number)
        def _(piece=piece):
            out[...] = piece[...]


def assemble(places, pieces):
    tokens, columns = pieces[0].shape
    return pl.pallas_call(
        assemble_kernel,
        grid_spec=pltpu.PrefetchScalarGridSpec(
            num_scalar_prefetch=1,
            grid=(len(pieces),),
            in_specs=[pl.BlockSpec((tokens, columns), lambda i, code: (0, 0))] * len(pieces),
            out_specs=pl.BlockSpec((tokens, columns), lambda i, code: (0, code[i])),
        ),
        out_shape=jax.ShapeDtypeStruct((tokens, columns * len(pieces)), pieces[0].dtype),
        compiler_params=pltpu.CompilerParams(vmem_limit_bytes=32 * 2**20),
    )(jnp.stack(places).astype(jnp.int32), *pieces)


class Held(dict):
    def gate(self, *names):
        names = list(dict.fromkeys(names))
        for name, value in zip(names, lax.optimization_barrier(tuple(self[n] for n in names))):
            self[name] = value

    def all(self, letter, numbers):
        return [self[letter, i] for i in numbers]


def fast_shards(hidden, base_weight, adapter_in, adapter_out, cotangent):
    feature_count = hidden.shape[1] * 2
    tokens, depth = hidden.shape
    columns = base_weight.shape[1]
    place = lax.axis_index("dp")
    z, member = place // GROUP, place % GROUP
    x, core = member // 2, member % 2
    y = lax.axis_index("tensor")
    outer = jnp.logical_or(z == 0, z == LINE - 1)
    inner = jnp.logical_not(outer)
    early = (z // 2) == y
    late = jnp.logical_not(early)
    side = jnp.where(z < 2, 0, 1)
    scale = jnp.float32(adapter_scale)
    parts, slots = 4, 3 * HALVES
    rows, step = depth // HALVES, tokens // parts
    held = Held()
    held["own", 0], held["x", 0] = base_weight[:rows], hidden[:step]
    held["weight"], held["hidden"] = base_weight, hidden

    def send_weight(s):
        hop = s // HALVES
        if hop == LINE - 2:
            far = [jnp.where(side == 0, held["left", q], held["right", q]) for q in (2, 3)]
            far.append(held["own", 1])
            sent = jnp.where(jnp.logical_and(early, inner), far[s - 3], far[s - 4])
            pairs = line_pairs([1], -1) + line_pairs([LINE - 2], 1)
            held["left", s] = held["right", s] = lax.ppermute(sent, "dp", pairs)
            return
        for name, sign, last in (("left", -1, 1), ("right", 1, LINE - 2)):
            sent = held["own", s] if s < HALVES else held[name, s - HALVES]
            if s > 0:
                other = held[name, s - 1]
                sent = jnp.where(jnp.logical_and(early, z == last), other, sent)
            sources = [q for q in range(LINE) if 0 <= q + sign < LINE and 0 <= q - sign * hop < LINE]
            held[name, s] = lax.ppermute(sent, "dp", line_pairs(sources, sign))

    def send_hidden(i):
        if i:
            held["x", i] = held["hidden"][i * step : (i + 1) * step]
        held["x", i] = lax.ppermute(held["x", i], "dp", x_swap)

    def over_core(name, result=None):
        held[result or name] = lax.ppermute(held[name], "dp", core_swap)

    def pass_hidden(i):
        over_core(("x", i), ("far", i))

    def send_sums(k):
        sent = lax.dynamic_index_in_dim(held["mine"], z ^ k, 0, False).astype(jnp.bfloat16)
        pairs = [(q * GROUP + r, (q ^ k) * GROUP + r) for q in range(LINE) for r in range(GROUP)]
        held["got", k] = lax.ppermute(sent, "dp", pairs)

    def codes(default, *cases):
        return pick(cases, default).astype(jnp.int32)[None]

    def streams(*numbers):
        return [(held[name, s], 0) for s in numbers for name in ("left", "right")]

    def window(s, *names):
        names = [("left", s), ("right", s), "weight", *names]
        held.gate(*names)
        held["own", 1] = held["weight"][rows:]
        if s < LINE - 1:
            send_weight(s + 1)
        if s == LINE - 1:
            send_weight(s + 1)
            send_weight(s + 2)

    end_early = jnp.logical_and(outer, early)
    end_late = jnp.logical_and(outer, late)
    inner_late = jnp.logical_and(inner, late)
    none = jnp.zeros((1,), jnp.int32)
    first_code = codes(2 + side, (end_early, side), (inner_late, 3 - side))
    first_code = jnp.concatenate([first_code] * HALVES)
    second_code = codes(4 + side, (end_early, side), (inner_late, 2 + side))
    second_code = jnp.concatenate([second_code] * HALVES)
    third_code = [
        codes(
            1 - side,
            (end_early, side + (0 if q == 0 else 2)),
            (end_late, 2 + side),
            (inner_late, 4 + side),
        )
        for q in range(HALVES)
    ]

    send_weight(0)
    send_hidden(0)
    held["core"] = lax.ppermute(hidden, "dp", core_swap)
    held["shared"] = shared_sums(hidden, adapter_in, cotangent, adapter_out)
    held["shared other"] = lax.ppermute(held["shared"], "tensor", pair_swap)
    rank = adapter_in.shape[0]
    share = rank // (LINE * GROUP)
    row = jnp.arange(rank)
    which = row // (LINE * share)
    owner = member ^ jnp.where(which == 0, 3, jnp.where(which == 1, 1, jnp.where(which == 2, 2, 0)))
    column = (row // share % LINE) * (GROUP * share) + owner * share + row % share
    held["order"] = (column[:, None] == jnp.arange(rank)[None, :]).astype(jnp.bfloat16)

    window(0, ("x", 0), "hidden")
    send_hidden(1)
    held["t", 0], held["sent"], held["kept"] = gradients(
        held["shared"], held["shared other"], held["order"], feature_count, hidden, cotangent
    )
    over_core("sent")

    window(1, ("x", 1), "hidden", "core", "kept", ("t", 0))
    send_hidden(2)
    pass_hidden(0)
    near = [hidden, held["core"]]
    whole_weight = [[(base_weight, 0)]]
    held["own sum", 0] = product(none, depth, whole_weight, near)

    window(2, ("x", 2), "hidden", ("far", 0), "sent", "kept", ("own sum", 0))
    send_hidden(3)
    pass_hidden(1)
    pass_hidden(2)
    sums = held["kept"] + held["sent"]
    flat = sums[: rank // 4].astype(jnp.bfloat16)
    held["sent"] = jnp.concatenate([flat, held["t", 0].reshape(flat.shape[0], -1)], axis=1)
    held["kept"] = sums[rank // 4 :]
    first = [streams(1 + q, q) for q in range(HALVES)]
    held["first sum", 0] = product(first_code, rows, first, near)

    held["y", 0] = jnp.where(early, held["first sum", 0], held["own sum", 0])

    window(3, ("x", 3), ("far", 1), ("far", 2), "sent", "kept", ("first sum", 0), ("y", 0))
    pass_hidden(3)
    held["sent"] = lax.ppermute(held["sent"], "dp", x_swap)
    held["y", 0] = lax.ppermute(held["y", 0], "tensor", pair_swap)
    half = parts // 2
    for h in (1, 2):
        pieces = range((h - 1) * half, h * half)
        members = held.all("x", pieces) + held.all("far", pieces)
        held["own sum", h] = product(none, depth, whole_weight, members)
        held["first sum", h] = product(first_code, rows, first, members)

    def in_order(name):
        a, b = held[name, 1], held[name, 2]
        cut = a.shape[0] // 2
        return jnp.concatenate([a[:cut], b[:cut], a[cut:], b[cut:]])

    first_sums = [held["first sum", 0], in_order("first sum")]
    own_sums = [held["own sum", 0], in_order("own sum")]
    held["y", 1] = lax.ppermute(
        jnp.where(early, first_sums[1], own_sums[1]), "tensor", pair_swap
    )

    far = held.all("x", range(parts)) + held.all("far", range(parts))
    groups = (near, far)
    second = [streams(3, 0, 2)]
    for h in range(2):
        held["half", h] = product(second_code[:1], rows, second, groups[h])
    width = held["kept"].shape[1]
    held["t", 2] = held["sent"][:, width:].reshape(tokens, -1)
    held["mine"] = held["kept"] + held["sent"][:, :width].astype(jnp.float32)
    held["mine"] = held["mine"].reshape(LINE, share, -1)

    window(4, "mine", ("t", 2), ("far", 3), ("y", 0), ("y", 1), ("t", 0), ("half", 0), ("half", 1))
    for m in (0, 2):
        held["t", m + 1] = held["t", m]
        over_core(("t", m + 1))
    for k in (1, 2, 3):
        send_sums(k)
    mixed = [streams(0, 4, 2), streams(4, 1, 3)]
    parity = (z % 2) ^ inner_late.astype(jnp.int32)
    blocks = [(parity ^ turn) * GROUP for turn in range(2)]
    factors = [
        lax.dynamic_slice_in_dim(adapter_out, (block + member) * columns, columns, 1)
        for block in blocks
    ]
    swaps = (None, core_swap, x_swap, both_swap)
    numbers = ((0, 1), (2, 3))
    places, pieces = [], []

    def give_out(turn, h, value):
        for i, m in reversed(list(enumerate(numbers[h]))):
            piece = value[i * tokens : (i + 1) * tokens]
            if m:
                piece = lax.ppermute(piece, "dp", swaps[m])
            places.append(blocks[turn] + (member ^ m))
            pieces.append(piece)

    group_tangents = [jnp.concatenate(held.all("t", numbers[h])) for h in range(2)]
    mixed_code = jnp.concatenate([third_code[0], second_code[1:], early.astype(jnp.int32)[None]])
    for h in (1, 0):
        extra = (
            held["half", h], first_sums[h], own_sums[h], held["y", h], group_tangents[h], factors[0]
        )
        held["w", h], held["total", h], held["third sum", h] = product(
            mixed_code, rows, mixed, groups[h], extra=extra, dtype=jnp.bfloat16
        )
        held["w", h] = lax.ppermute(held["w", h], "tensor", pair_swap)
    for h in (1, 0):
        give_out(0, h, held["total", h])

    window(5, ("third sum", 0), ("third sum", 1))
    for h in (1, 0):
        chunk = [streams(1, 5, 3)]
        extra = (held["third sum", h], held["w", h], group_tangents[h], factors[1])
        value = product(third_code[1], rows, chunk, groups[h], rows, extra, jnp.bfloat16)
        give_out(1, h, value)
    output = assemble(places, pieces)
    grads = lax.dynamic_index_in_dim(held["mine"], z, 0, False)
    held["grads"] = sum((held["got", k].astype(jnp.float32) for k in (1, 2, 3)), grads)
    return (output, held["grads"][:, :depth], held["grads"][:, depth:])


def solution(mesh):
    fits = mesh.shape["dp"] == LINE * GROUP and mesh.shape["tensor"] == 2
    return jax.shard_map(
        fast_shards if fits else plain_shards,
        mesh=mesh,
        in_specs=(
            P("dp", "tensor"),
            P("tensor", "dp"),
            P(None, "tensor"),
            P(None, "tensor"),
            P("dp", "tensor"),
        ),
        out_specs=(P("dp", "tensor"), P("dp", "tensor"), P("dp", "tensor")),
        check_vma=False,
    )
```

```python
import functools

import jax
import jax.numpy as jnp
from jax import lax
from jax.experimental import pallas as pl
from jax.experimental.pallas import tpu as pltpu
from jax.sharding import PartitionSpec as P

adapter_scale = 4.0
exp_rate = 0.25
tiny_eps = 1e-06


def inverse_sinh(value):
    return jnp.log(value + jnp.sqrt(1.0 + value * value))


def plain_shards(hidden, base_weight, adapter_in, adapter_out, cotangent):
    feature_count = hidden.shape[1] * lax.axis_size("tensor")
    contract_last = (((1,), (1,)), ((), ()))
    contract_first = (((0,), (0,)), ((), ()))
    square_part = jnp.sum(jnp.square(hidden.astype(jnp.float32)), axis=1)
    rank_part = lax.dot_general(
        hidden, adapter_in, contract_last, preferred_element_type=jnp.float32
    )
    square_sum, lorentz_raw = lax.psum((square_part, rank_part), "tensor")
    level = jnp.sqrt(square_sum / feature_count + tiny_eps)
    radius = exp_rate * level
    lift_factor = jnp.sinh(radius) / radius
    lorentz = lift_factor[:, None] * lorentz_raw
    norm_value = jnp.sqrt(jnp.sum(lorentz * lorentz, axis=1) + tiny_eps)
    phi_value = inverse_sinh(norm_value) / norm_value
    tangent = (phi_value[:, None] * lorentz).astype(jnp.bfloat16)
    partial_cols = jnp.dot(
        hidden,
        lax.all_gather(base_weight, "dp", axis=1, tiled=True),
        preferred_element_type=jnp.float32,
    )
    base_sum = lax.psum_scatter(partial_cols, "tensor", scatter_dimension=1, tiled=True)
    adapter_term = jnp.dot(tangent, adapter_out, preferred_element_type=jnp.float32)
    output = (base_sum + adapter_scale * adapter_term).astype(jnp.bfloat16)
    out_part = adapter_scale * lax.dot_general(
        tangent, cotangent, contract_first, preferred_element_type=jnp.float32
    )
    cotan_later = adapter_scale * lax.dot_general(
        cotangent, adapter_out, contract_last, preferred_element_type=jnp.float32
    )
    tangent_grad = lax.psum(cotan_later, "tensor")
    inner_value = jnp.sum(lorentz * tangent_grad, axis=1)
    coefficient = (1.0 / jnp.sqrt(1.0 + norm_value * norm_value) - phi_value) / (
        norm_value * norm_value
    )
    lorentz_grad = (
        phi_value[:, None] * tangent_grad + (coefficient * inner_value)[:, None] * lorentz
    )
    raw_grad = (lift_factor[:, None] * lorentz_grad).astype(jnp.bfloat16)
    in_part = lax.dot_general(raw_grad, hidden, contract_first, preferred_element_type=jnp.float32)
    grad_in, grad_out = (
        lax.psum_scatter(in_part, "dp", scatter_dimension=0, tiled=True),
        lax.psum_scatter(out_part, "dp", scatter_dimension=0, tiled=True),
    )
    return (output, grad_in, grad_out)


GROUP = 4
LINE = 4
HALVES = 2
core_swap = [(d, d ^ 1) for d in range(LINE * GROUP)]
x_swap = [(d, d ^ 2) for d in range(LINE * GROUP)]
both_swap = [(d, d ^ 3) for d in range(LINE * GROUP)]
pair_swap = [(0, 1), (1, 0)]


def line_pairs(sources, step):
    return [(z * GROUP + r, (z + step) * GROUP + r) for z in sources for r in range(GROUP)]


def pick(cases, default):
    out = default
    for condition, value in cases:
        out = jnp.where(condition, value, out)
    return out


def dot32(a, b):
    return jnp.dot(a, b, preferred_element_type=jnp.float32)


ROWS = 256
COST = 0.01


def product_kernel(plan, sources, blocks, has_base, *refs):
    code, refs = refs[0], refs[1:]
    weights, refs = refs[: sources[0]], refs[sources[0] :]
    hiddens, refs = refs[: sources[1]], refs[sources[1] :]
    extra, refs = refs[:has_base], refs[has_base:]
    outs, (weight, slots, weight_sem, slot_sems) = refs[:-4], refs[-4:]
    out = outs[0]
    first_column = plan[1]
    depth = weight.shape[0]
    step = depth // len(plan[0])

    def weight_copy(c, candidate):
        source, row = candidate
        return pltpu.make_async_copy(
            weights[source].at[pl.ds(row, step)],
            weight.at[pl.ds(c * step, step)],
            weight_sem.at[c],
        )

    def hidden_copies(b):
        copies, at = [], 0
        for source, row, rows in blocks[b]:
            copies.append(
                pltpu.make_async_copy(
                    hiddens[source].at[pl.ds(row, rows), pl.ds(first_column, depth)],
                    slots.at[b % 2, pl.ds(at, rows)],
                    slot_sems.at[b % 2],
                )
            )
            at += rows
        return copies

    for copy in hidden_copies(0):
        copy.start()
    for c, candidates in enumerate(plan[0]):
        if len(candidates) == 1:
            weight_copy(c, candidates[0]).start()
        for number, candidate in enumerate(candidates if len(candidates) > 1 else ()):

            @pl.when(code[c] == number)
            def _(c=c, candidate=candidate):
                weight_copy(c, candidate).start()

    for copy in hidden_copies(1):
        copy.start()
    for c, candidates in enumerate(plan[0]):
        weight_copy(c, candidates[0]).wait()

    def body(b, carry):
        slot = lax.rem(b, 2)
        for number in range(len(blocks)):

            @pl.when(b == number)
            def _(number=number):
                for copy in hidden_copies(number):
                    copy.wait()

        rows = pl.ds(pl.multiple_of(b * ROWS, ROWS), ROWS)
        if len(extra) == 6:
            third = jnp.dot(
                slots[slot, :, :step], weight[:step], preferred_element_type=jnp.float32
            )
            outs[2][rows, :] = third
            total = extra[0][rows, :] + jnp.dot(
                slots[slot, :, step:], weight[step:], preferred_element_type=jnp.float32
            )
        else:
            total = jnp.dot(slots[slot], weight[...], preferred_element_type=jnp.float32)
        if len(extra) > 0:
            other, tangent, factor = extra[-3:]
            term = jnp.dot(tangent[rows, :], factor[...], preferred_element_type=jnp.float32)
            term = other[rows, :].astype(jnp.float32) + jnp.float32(adapter_scale) * term
        if len(extra) == 6:
            gives = code[len(plan[0])] == 1
            first, own = extra[1][rows, :], extra[2][rows, :]
            outs[1][rows, :] = (jnp.where(gives, own, total) + term).astype(outs[1].dtype)
            total = jnp.where(gives, total, first)
        elif len(extra) == 4:
            total = total + extra[0][rows, :] + term
        out[rows, :] = total.astype(out.dtype)
        for number in range(2, len(blocks)):

            @pl.when(b + 2 == number)
            def _(number=number):
                for copy in hidden_copies(number):
                    copy.start()

        return carry

    lax.fori_loop(0, len(blocks), body, 0)


def product(code, step, chunks, hiddens, first_column=0, extra=(), dtype=jnp.float32):
    weights, candidates = [], []
    for chunk in chunks:
        for array, _ in chunk:
            if not any(array is weight for weight in weights):
                weights.append(array)
        candidates.append(
            tuple(
                ([array is weight for weight in weights].index(True), row) for array, row in chunk
            )
        )
    depth = step * len(chunks)
    columns = weights[0].shape[1]
    blocks, room = [], 0
    for number, array in enumerate(hiddens):
        row = 0
        while row < array.shape[0]:
            if room == 0:
                blocks.append([])
                room = ROWS
            rows = min(room, array.shape[0] - row)
            blocks[-1].append((number, row, rows))
            row, room = row + rows, room - rows
    height = len(blocks) * ROWS
    anywhere = pl.BlockSpec(memory_space=pl.ANY)
    whole = pl.BlockSpec(memory_space=pltpu.VMEM)
    operands = [code, *weights, *hiddens, *extra]
    in_specs = [pl.BlockSpec(memory_space=pltpu.SMEM)]
    in_specs += [anywhere] * (len(weights) + len(hiddens)) + [whole] * len(extra)
    kernel = functools.partial(
        product_kernel,
        (tuple(candidates), first_column),
        (len(weights), len(hiddens)),
        blocks,
        len(extra),
    )
    shape = jax.ShapeDtypeStruct((height, columns), dtype)
    shapes = (shape, shape, jax.ShapeDtypeStruct((height, columns), jnp.float32))
    several = len(extra) == 6
    return pl.pallas_call(
        kernel,
        out_shape=shapes if several else shape,
        in_specs=in_specs,
        out_specs=(whole,) * 3 if several else whole,
        scratch_shapes=[
            pltpu.VMEM((depth, columns), jnp.bfloat16),
            pltpu.VMEM((2, ROWS, depth), jnp.bfloat16),
            pltpu.SemaphoreType.DMA((len(chunks),)),
            pltpu.SemaphoreType.DMA((2,)),
        ],
        compiler_params=pltpu.CompilerParams(vmem_limit_bytes=40 * 2**20),
        cost_estimate=pl.CostEstimate(
            flops=int(2 * height * depth * columns * COST),
            bytes_accessed=int(2 * depth * (height + columns) * COST),
            transcendentals=0,
        ),
    )(*operands)


TILE = 1024
LANES = 128


def shared_kernel(in_steps, hidden, adapter_in, cotangent, adapter_out, out):
    number = pl.program_id(0)
    rank = adapter_in.shape[0]
    contract_last = (((1,), (1,)), ((), ()))

    @pl.when(number == 0)
    def _():
        out[...] = jnp.zeros_like(out)

    @pl.when(number < in_steps)
    def _():
        rows = hidden[...]
        out[:, :rank] += lax.dot_general(
            rows, adapter_in[...], contract_last, preferred_element_type=jnp.float32
        )
        wide = rows.astype(jnp.float32)
        squares = jnp.sum(wide * wide, axis=1, keepdims=True)
        out[:, 2 * rank :] += jnp.broadcast_to(squares, (rows.shape[0], LANES))

    @pl.when(number >= in_steps)
    def _():
        out[:, rank : 2 * rank] += adapter_scale * lax.dot_general(
            cotangent[...], adapter_out[...], contract_last, preferred_element_type=jnp.float32
        )


def shared_sums(hidden, adapter_in, cotangent, adapter_out):
    tokens, rank = hidden.shape[0], adapter_in.shape[0]
    in_steps, out_steps = hidden.shape[1] // TILE, cotangent.shape[1] // TILE
    early = lambda i: (0, jnp.minimum(i, in_steps - 1))
    late = lambda i: (0, jnp.maximum(i - in_steps, 0))
    return pl.pallas_call(
        functools.partial(shared_kernel, in_steps),
        grid=(in_steps + out_steps,),
        out_shape=jax.ShapeDtypeStruct((tokens, 2 * rank + LANES), jnp.float32),
        in_specs=[
            pl.BlockSpec((tokens, TILE), early),
            pl.BlockSpec((rank, TILE), early),
            pl.BlockSpec((tokens, TILE), late),
            pl.BlockSpec((rank, TILE), late),
        ],
        out_specs=pl.BlockSpec((tokens, 2 * rank + LANES), lambda i: (0, 0)),
        compiler_params=pltpu.CompilerParams(vmem_limit_bytes=32 * 2**20),
        cost_estimate=pl.CostEstimate(
            flops=int(2 * tokens * rank * TILE * (in_steps + out_steps) * COST),
            bytes_accessed=int(2 * TILE * (tokens + rank) * (in_steps + out_steps) * COST),
            transcendentals=0,
        ),
    )(hidden, adapter_in, cotangent, adapter_out)


def lift_of(radius):
    square = radius * radius
    series = 1.0 + square / 6.0 * (
        1.0 + square / 20.0 * (1.0 + square / 42.0 * (1.0 + square / 72.0))
    )
    large = (jnp.exp(radius) - jnp.exp(-radius)) * 0.5 / radius
    return jnp.where(radius < 1.0, series, large)


def gradient_kernel(
    in_steps, feature_count, own, other, order, hidden, cotangent, tangent_out, sent, kept, left_in, left_out
):
    number = pl.program_id(0)
    rank, half = order.shape[0], sent.shape[0]

    @pl.when(number == 0)
    def _():
        total = own[...] + other[...]
        raw, tangent_grad = total[:, :rank], total[:, rank : 2 * rank]
        square_sum = total[:, 2 * rank : 2 * rank + 1]
        level = jnp.sqrt(square_sum / feature_count + tiny_eps)
        lift_factor = lift_of(exp_rate * level)
        lorentz = lift_factor * raw
        norm_value = jnp.sqrt(jnp.sum(lorentz * lorentz, axis=1, keepdims=True) + tiny_eps)
        phi_value = inverse_sinh(norm_value) / norm_value
        tangent = (phi_value * lorentz).astype(jnp.bfloat16)
        inner_value = jnp.sum(lorentz * tangent_grad, axis=1, keepdims=True)
        coefficient = (1.0 / jnp.sqrt(1.0 + norm_value * norm_value) - phi_value) / (
            norm_value * norm_value
        )
        lorentz_grad = phi_value * tangent_grad + (coefficient * inner_value) * lorentz
        raw_grad = (lift_factor * lorentz_grad).astype(jnp.bfloat16)
        tangent_out[...] = tangent
        contract_last = (((1,), (1,)), ((), ()))
        for target, value in ((left_in, raw_grad), (left_out, tangent)):
            target[...] = lax.dot_general(
                order[...], value, contract_last, preferred_element_type=jnp.float32
            ).astype(jnp.bfloat16)

    @pl.when(number < in_steps)
    def _():
        total = jnp.dot(left_in[...], hidden[...], preferred_element_type=jnp.float32)
        sent[...] = total[:half]
        kept[...] = total[half:]

    @pl.when(number >= in_steps)
    def _():
        total = adapter_scale * jnp.dot(
            left_out[...], cotangent[...], preferred_element_type=jnp.float32
        )
        sent[...] = total[:half]
        kept[...] = total[half:]


def gradients(own, other, order, feature_count, hidden, cotangent):
    rank, tokens = order.shape[0], hidden.shape[0]
    in_steps, out_steps = hidden.shape[1] // TILE, cotangent.shape[1] // TILE
    steps = in_steps + out_steps
    shape = jax.ShapeDtypeStruct((rank // 2, steps * TILE), jnp.float32)
    part = pl.BlockSpec((rank // 2, TILE), lambda i: (0, i))
    return pl.pallas_call(
        functools.partial(gradient_kernel, in_steps, feature_count),
        grid=(steps,),
        out_shape=(jax.ShapeDtypeStruct((tokens, rank), jnp.bfloat16), shape, shape),
        in_specs=[
            pl.BlockSpec(own.shape, lambda i: (0, 0)),
            pl.BlockSpec(own.shape, lambda i: (0, 0)),
            pl.BlockSpec(order.shape, lambda i: (0, 0)),
            pl.BlockSpec((tokens, TILE), lambda i: (0, jnp.minimum(i, in_steps - 1))),
            pl.BlockSpec((tokens, TILE), lambda i: (0, jnp.maximum(i - in_steps, 0))),
        ],
        out_specs=(pl.BlockSpec((tokens, rank), lambda i: (0, 0)), part, part),
        scratch_shapes=[pltpu.VMEM((rank, tokens), jnp.bfloat16)] * 2,
        compiler_params=pltpu.CompilerParams(vmem_limit_bytes=32 * 2**20),
        cost_estimate=pl.CostEstimate(
            flops=int(2 * rank * tokens * steps * TILE * COST),
            bytes_accessed=int((2 * tokens + 4 * rank) * steps * TILE * COST),
            transcendentals=0,
        ),
    )(own, other, order, hidden, cotangent)


def assemble_kernel(code, *refs):
    out = refs[-1]
    for number, piece in enumerate(refs[:-1]):

        @pl.when(pl.program_id(0) == number)
        def _(piece=piece):
            out[...] = piece[...]


def assemble(places, pieces):
    tokens, columns = pieces[0].shape
    return pl.pallas_call(
        assemble_kernel,
        grid_spec=pltpu.PrefetchScalarGridSpec(
            num_scalar_prefetch=1,
            grid=(len(pieces),),
            in_specs=[pl.BlockSpec((tokens, columns), lambda i, code: (0, 0))] * len(pieces),
            out_specs=pl.BlockSpec((tokens, columns), lambda i, code: (0, code[i])),
        ),
        out_shape=jax.ShapeDtypeStruct((tokens, columns * len(pieces)), pieces[0].dtype),
        compiler_params=pltpu.CompilerParams(vmem_limit_bytes=32 * 2**20),
    )(jnp.stack(places).astype(jnp.int32), *pieces)


class Held(dict):
    def gate(self, *names):
        names = list(dict.fromkeys(names))
        for name, value in zip(names, lax.optimization_barrier(tuple(self[n] for n in names))):
            self[name] = value

    def all(self, letter, numbers):
        return [self[letter, i] for i in numbers]


def fast_shards(hidden, base_weight, adapter_in, adapter_out, cotangent):
    feature_count = hidden.shape[1] * 2
    tokens, depth = hidden.shape
    columns = base_weight.shape[1]
    place = lax.axis_index("dp")
    z, member = place // GROUP, place % GROUP
    x, core = member // 2, member % 2
    y = lax.axis_index("tensor")
    outer = jnp.logical_or(z == 0, z == LINE - 1)
    inner = jnp.logical_not(outer)
    early = (z // 2) == y
    late = jnp.logical_not(early)
    side = jnp.where(z < 2, 0, 1)
    scale = jnp.float32(adapter_scale)
    parts, slots = 4, 3 * HALVES
    rows, step = depth // HALVES, tokens // parts
    held = Held()
    held["own", 0], held["x", 0] = base_weight[:rows], hidden[:step]
    held["weight"], held["hidden"] = base_weight, hidden

    def send_weight(s):
        hop = s // HALVES
        if hop == LINE - 2:
            far = [jnp.where(side == 0, held["left", q], held["right", q]) for q in (2, 3)]
            far.append(held["own", 1])
            sent = jnp.where(jnp.logical_and(early, inner), far[s - 3], far[s - 4])
            pairs = line_pairs([1], -1) + line_pairs([LINE - 2], 1)
            held["left", s] = held["right", s] = lax.ppermute(sent, "dp", pairs)
            return
        for name, sign, last in (("left", -1, 1), ("right", 1, LINE - 2)):
            sent = held["own", s] if s < HALVES else held[name, s - HALVES]
            if s > 0:
                other = held[name, s - 1]
                sent = jnp.where(jnp.logical_and(early, z == last), other, sent)
            sources = [q for q in range(LINE) if 0 <= q + sign < LINE and 0 <= q - sign * hop < LINE]
            held[name, s] = lax.ppermute(sent, "dp", line_pairs(sources, sign))

    def send_hidden(i):
        held["x", i] = lax.ppermute(held["x", i], "dp", x_swap)
        if i + 1 < parts:
            held["x", i + 1] = held["hidden"][(i + 1) * step : (i + 2) * step]

    def over_core(name, result=None):
        held[result or name] = lax.ppermute(held[name], "dp", core_swap)

    def pass_hidden(i):
        over_core(("x", i), ("far", i))

    def send_sums(k):
        sent = lax.dynamic_index_in_dim(held["mine"], z ^ k, 0, False).astype(jnp.bfloat16)
        pairs = [(q * GROUP + r, (q ^ k) * GROUP + r) for q in range(LINE) for r in range(GROUP)]
        held["got", k] = lax.ppermute(sent, "dp", pairs)

    def codes(default, *cases):
        return pick(cases, default).astype(jnp.int32)[None]

    def streams(*numbers):
        return [(held[name, s], 0) for s in numbers for name in ("left", "right")]

    def window(s, *names):
        names = [("left", s), ("right", s), "weight", *names]
        held.gate(*names)
        held["own", 1] = held["weight"][rows:]
        if s < LINE - 1:
            send_weight(s + 1)
        if s == LINE - 1:
            send_weight(s + 1)
            send_weight(s + 2)

    end_early = jnp.logical_and(outer, early)
    end_late = jnp.logical_and(outer, late)
    inner_late = jnp.logical_and(inner, late)
    none = jnp.zeros((1,), jnp.int32)
    first_code = codes(2 + side, (end_early, side), (inner_late, 3 - side))
    first_code = jnp.concatenate([first_code] * HALVES)
    second_code = codes(4 + side, (end_early, side), (inner_late, 2 + side))
    second_code = jnp.concatenate([second_code] * HALVES)
    third_code = [
        codes(
            1 - side,
            (end_early, side + (0 if q == 0 else 2)),
            (end_late, 2 + side),
            (inner_late, 4 + side),
        )
        for q in range(HALVES)
    ]

    send_weight(0)
    send_hidden(0)
    held["core"] = lax.ppermute(hidden, "dp", core_swap)
    held["shared"] = shared_sums(hidden, adapter_in, cotangent, adapter_out)
    held["shared other"] = lax.ppermute(held["shared"], "tensor", pair_swap)
    rank = adapter_in.shape[0]
    share = rank // (LINE * GROUP)
    row = jnp.arange(rank)
    which = row // (LINE * share)
    owner = member ^ jnp.where(which == 0, 3, jnp.where(which == 1, 1, jnp.where(which == 2, 2, 0)))
    column = (row // share % LINE) * (GROUP * share) + owner * share + row % share
    held["order"] = (column[:, None] == jnp.arange(rank)[None, :]).astype(jnp.bfloat16)

    window(0, ("x", 0), ("x", 1), "hidden")
    send_hidden(1)
    held["t", 0], held["sent"], held["kept"] = gradients(
        held["shared"], held["shared other"], held["order"], feature_count, hidden, cotangent
    )
    over_core("sent")

    window(1, ("x", 1), ("x", 2), "hidden", "core", "kept", ("t", 0))
    send_hidden(2)
    pass_hidden(0)
    near = [hidden, held["core"]]
    whole_weight = [[(base_weight, 0)]]
    held["own sum", 0] = product(none, depth, whole_weight, near)

    window(2, ("x", 2), ("x", 3), ("far", 0), "sent", "kept", ("own sum", 0))
    send_hidden(3)
    pass_hidden(1)
    pass_hidden(2)
    sums = held["kept"] + held["sent"]
    flat = sums[: rank // 4].astype(jnp.bfloat16)
    held["sent"] = jnp.concatenate([flat, held["t", 0].reshape(flat.shape[0], -1)], axis=1)
    held["kept"] = sums[rank // 4 :]
    first = [streams(1 + q, q) for q in range(HALVES)]
    held["first sum", 0] = product(first_code, rows, first, near)

    held["y", 0] = jnp.where(early, held["first sum", 0], held["own sum", 0])

    window(3, ("x", 3), ("far", 1), ("far", 2), "sent", "kept", ("first sum", 0), ("y", 0))
    pass_hidden(3)
    held["sent"] = lax.ppermute(held["sent"], "dp", x_swap)
    held["y", 0] = lax.ppermute(held["y", 0], "tensor", pair_swap)
    half = parts // 2
    for h in (1, 2):
        pieces = range((h - 1) * half, h * half)
        members = held.all("x", pieces) + held.all("far", pieces)
        held["own sum", h] = product(none, depth, whole_weight, members)
        held["first sum", h] = product(first_code, rows, first, members)

    def in_order(name):
        a, b = held[name, 1], held[name, 2]
        cut = a.shape[0] // 2
        return jnp.concatenate([a[:cut], b[:cut], a[cut:], b[cut:]])

    first_sums = [held["first sum", 0], in_order("first sum")]
    own_sums = [held["own sum", 0], in_order("own sum")]
    held["y", 1] = lax.ppermute(
        jnp.where(early, first_sums[1], own_sums[1]), "tensor", pair_swap
    )

    far = held.all("x", range(parts)) + held.all("far", range(parts))
    groups = (near, far)
    second = [streams(3, 0, 2)]
    for h in range(2):
        held["half", h] = product(second_code[:1], rows, second, groups[h])
    width = held["kept"].shape[1]
    held["t", 2] = held["sent"][:, width:].reshape(tokens, -1)
    held["mine"] = held["kept"] + held["sent"][:, :width].astype(jnp.float32)
    held["mine"] = held["mine"].reshape(LINE, share, -1)

    window(4, "mine", ("t", 2), ("far", 3), ("y", 0), ("y", 1), ("t", 0), ("half", 0), ("half", 1))
    for m in (0, 2):
        held["t", m + 1] = held["t", m]
        over_core(("t", m + 1))
    for k in (1, 2, 3):
        send_sums(k)
    mixed = [streams(0, 4, 2), streams(4, 1, 3)]
    parity = (z % 2) ^ inner_late.astype(jnp.int32)
    blocks = [(parity ^ turn) * GROUP for turn in range(2)]
    factors = [
        lax.dynamic_slice_in_dim(adapter_out, (block + member) * columns, columns, 1)
        for block in blocks
    ]
    swaps = (None, core_swap, x_swap, both_swap)
    numbers = ((0, 1), (2, 3))
    places, pieces = [], []

    def give_out(turn, h, value):
        for i, m in reversed(list(enumerate(numbers[h]))):
            piece = value[i * tokens : (i + 1) * tokens]
            if m:
                piece = lax.ppermute(piece, "dp", swaps[m])
            places.append(blocks[turn] + (member ^ m))
            pieces.append(piece)

    group_tangents = [jnp.concatenate(held.all("t", numbers[h])) for h in range(2)]
    mixed_code = jnp.concatenate([third_code[0], second_code[1:], early.astype(jnp.int32)[None]])
    for h in (1, 0):
        extra = (
            held["half", h], first_sums[h], own_sums[h], held["y", h], group_tangents[h], factors[0]
        )
        held["w", h], held["total", h], held["third sum", h] = product(
            mixed_code, rows, mixed, groups[h], extra=extra, dtype=jnp.bfloat16
        )
        held["w", h] = lax.ppermute(held["w", h], "tensor", pair_swap)
    for h in (1, 0):
        give_out(0, h, held["total", h])

    window(5, ("third sum", 0), ("third sum", 1))
    for h in (1, 0):
        chunk = [streams(1, 5, 3)]
        extra = (held["third sum", h], held["w", h], group_tangents[h], factors[1])
        value = product(third_code[1], rows, chunk, groups[h], rows, extra, jnp.bfloat16)
        give_out(1, h, value)
    output = assemble(places, pieces)
    grads = lax.dynamic_index_in_dim(held["mine"], z, 0, False)
    held["grads"] = sum((held["got", k].astype(jnp.float32) for k in (1, 2, 3)), grads)
    return (output, held["grads"][:, :depth], held["grads"][:, depth:])


def solution(mesh):
    fits = mesh.shape["dp"] == LINE * GROUP and mesh.shape["tensor"] == 2
    return jax.shard_map(
        fast_shards if fits else plain_shards,
        mesh=mesh,
        in_specs=(
            P("dp", "tensor"),
            P("tensor", "dp"),
            P(None, "tensor"),
            P(None, "tensor"),
            P("dp", "tensor"),
        ),
        out_specs=(P("dp", "tensor"), P("dp", "tensor"), P("dp", "tensor")),
        check_vma=False,
    )
```

```python
import functools

import jax
import jax.numpy as jnp
from jax import lax
from jax.experimental import pallas as pl
from jax.experimental.pallas import tpu as pltpu
from jax.sharding import PartitionSpec as P

adapter_scale = 4.0
exp_rate = 0.25
tiny_eps = 1e-06


def inverse_sinh(value):
    return jnp.log(value + jnp.sqrt(1.0 + value * value))


def plain_shards(hidden, base_weight, adapter_in, adapter_out, cotangent):
    feature_count = hidden.shape[1] * lax.axis_size("tensor")
    contract_last = (((1,), (1,)), ((), ()))
    contract_first = (((0,), (0,)), ((), ()))
    square_part = jnp.sum(jnp.square(hidden.astype(jnp.float32)), axis=1)
    rank_part = lax.dot_general(
        hidden, adapter_in, contract_last, preferred_element_type=jnp.float32
    )
    square_sum, lorentz_raw = lax.psum((square_part, rank_part), "tensor")
    level = jnp.sqrt(square_sum / feature_count + tiny_eps)
    radius = exp_rate * level
    lift_factor = jnp.sinh(radius) / radius
    lorentz = lift_factor[:, None] * lorentz_raw
    norm_value = jnp.sqrt(jnp.sum(lorentz * lorentz, axis=1) + tiny_eps)
    phi_value = inverse_sinh(norm_value) / norm_value
    tangent = (phi_value[:, None] * lorentz).astype(jnp.bfloat16)
    partial_cols = jnp.dot(
        hidden,
        lax.all_gather(base_weight, "dp", axis=1, tiled=True),
        preferred_element_type=jnp.float32,
    )
    base_sum = lax.psum_scatter(partial_cols, "tensor", scatter_dimension=1, tiled=True)
    adapter_term = jnp.dot(tangent, adapter_out, preferred_element_type=jnp.float32)
    output = (base_sum + adapter_scale * adapter_term).astype(jnp.bfloat16)
    out_part = adapter_scale * lax.dot_general(
        tangent, cotangent, contract_first, preferred_element_type=jnp.float32
    )
    cotan_later = adapter_scale * lax.dot_general(
        cotangent, adapter_out, contract_last, preferred_element_type=jnp.float32
    )
    tangent_grad = lax.psum(cotan_later, "tensor")
    inner_value = jnp.sum(lorentz * tangent_grad, axis=1)
    coefficient = (1.0 / jnp.sqrt(1.0 + norm_value * norm_value) - phi_value) / (
        norm_value * norm_value
    )
    lorentz_grad = (
        phi_value[:, None] * tangent_grad + (coefficient * inner_value)[:, None] * lorentz
    )
    raw_grad = (lift_factor[:, None] * lorentz_grad).astype(jnp.bfloat16)
    in_part = lax.dot_general(raw_grad, hidden, contract_first, preferred_element_type=jnp.float32)
    grad_in, grad_out = (
        lax.psum_scatter(in_part, "dp", scatter_dimension=0, tiled=True),
        lax.psum_scatter(out_part, "dp", scatter_dimension=0, tiled=True),
    )
    return (output, grad_in, grad_out)


GROUP = 4
LINE = 4
HALVES = 2
core_swap = [(d, d ^ 1) for d in range(LINE * GROUP)]
x_swap = [(d, d ^ 2) for d in range(LINE * GROUP)]
both_swap = [(d, d ^ 3) for d in range(LINE * GROUP)]
pair_swap = [(0, 1), (1, 0)]


def line_pairs(sources, step):
    return [(z * GROUP + r, (z + step) * GROUP + r) for z in sources for r in range(GROUP)]


def pick(cases, default):
    out = default
    for condition, value in cases:
        out = jnp.where(condition, value, out)
    return out


def dot32(a, b):
    return jnp.dot(a, b, preferred_element_type=jnp.float32)


ROWS = 256
COST = 0.01


def product_kernel(plan, sources, blocks, has_base, *refs):
    code, refs = refs[0], refs[1:]
    weights, refs = refs[: sources[0]], refs[sources[0] :]
    hiddens, refs = refs[: sources[1]], refs[sources[1] :]
    extra, refs = refs[:has_base], refs[has_base:]
    outs, (weight, slots, weight_sem, slot_sems) = refs[:-4], refs[-4:]
    out = outs[0]
    first_column = plan[1]
    depth = weight.shape[0]
    step = depth // len(plan[0])

    def weight_copy(c, candidate):
        source, row = candidate
        return pltpu.make_async_copy(
            weights[source].at[pl.ds(row, step)],
            weight.at[pl.ds(c * step, step)],
            weight_sem.at[c],
        )

    def hidden_copies(b):
        copies, at = [], 0
        for source, row, rows in blocks[b]:
            copies.append(
                pltpu.make_async_copy(
                    hiddens[source].at[pl.ds(row, rows), pl.ds(first_column, depth)],
                    slots.at[b % 2, pl.ds(at, rows)],
                    slot_sems.at[b % 2],
                )
            )
            at += rows
        return copies

    for copy in hidden_copies(0):
        copy.start()
    for c, candidates in enumerate(plan[0]):
        if len(candidates) == 1:
            weight_copy(c, candidates[0]).start()
        for number, candidate in enumerate(candidates if len(candidates) > 1 else ()):

            @pl.when(code[c] == number)
            def _(c=c, candidate=candidate):
                weight_copy(c, candidate).start()

    for copy in hidden_copies(1):
        copy.start()
    for c, candidates in enumerate(plan[0]):
        weight_copy(c, candidates[0]).wait()

    def body(b, carry):
        slot = lax.rem(b, 2)
        for number in range(len(blocks)):

            @pl.when(b == number)
            def _(number=number):
                for copy in hidden_copies(number):
                    copy.wait()

        rows = pl.ds(pl.multiple_of(b * ROWS, ROWS), ROWS)
        if len(extra) == 6:
            third = jnp.dot(
                slots[slot, :, :step], weight[:step], preferred_element_type=jnp.float32
            )
            outs[2][rows, :] = third
            total = extra[0][rows, :] + jnp.dot(
                slots[slot, :, step:], weight[step:], preferred_element_type=jnp.float32
            )
        else:
            total = jnp.dot(slots[slot], weight[...], preferred_element_type=jnp.float32)
        if len(extra) > 0:
            other, tangent, factor = extra[-3:]
            term = jnp.dot(tangent[rows, :], factor[...], preferred_element_type=jnp.float32)
            term = other[rows, :].astype(jnp.float32) + jnp.float32(adapter_scale) * term
        if len(extra) == 6:
            gives = code[len(plan[0])] == 1
            first, own = extra[1][rows, :], extra[2][rows, :]
            outs[1][rows, :] = (jnp.where(gives, own, total) + term).astype(outs[1].dtype)
            total = jnp.where(gives, total, first)
        elif len(extra) == 4:
            total = total + extra[0][rows, :] + term
        out[rows, :] = total.astype(out.dtype)
        for number in range(2, len(blocks)):

            @pl.when(b + 2 == number)
            def _(number=number):
                for copy in hidden_copies(number):
                    copy.start()

        return carry

    lax.fori_loop(0, len(blocks), body, 0)


def product(code, step, chunks, hiddens, first_column=0, extra=(), dtype=jnp.float32):
    weights, candidates = [], []
    for chunk in chunks:
        for array, _ in chunk:
            if not any(array is weight for weight in weights):
                weights.append(array)
        candidates.append(
            tuple(
                ([array is weight for weight in weights].index(True), row) for array, row in chunk
            )
        )
    depth = step * len(chunks)
    columns = weights[0].shape[1]
    blocks, room = [], 0
    for number, array in enumerate(hiddens):
        row = 0
        while row < array.shape[0]:
            if room == 0:
                blocks.append([])
                room = ROWS
            rows = min(room, array.shape[0] - row)
            blocks[-1].append((number, row, rows))
            row, room = row + rows, room - rows
    height = len(blocks) * ROWS
    anywhere = pl.BlockSpec(memory_space=pl.ANY)
    whole = pl.BlockSpec(memory_space=pltpu.VMEM)
    operands = [code, *weights, *hiddens, *extra]
    in_specs = [pl.BlockSpec(memory_space=pltpu.SMEM)]
    in_specs += [anywhere] * (len(weights) + len(hiddens)) + [whole] * len(extra)
    kernel = functools.partial(
        product_kernel,
        (tuple(candidates), first_column),
        (len(weights), len(hiddens)),
        blocks,
        len(extra),
    )
    shape = jax.ShapeDtypeStruct((height, columns), dtype)
    shapes = (shape, shape, jax.ShapeDtypeStruct((height, columns), jnp.float32))
    several = len(extra) == 6
    return pl.pallas_call(
        kernel,
        out_shape=shapes if several else shape,
        in_specs=in_specs,
        out_specs=(whole,) * 3 if several else whole,
        scratch_shapes=[
            pltpu.VMEM((depth, columns), jnp.bfloat16),
            pltpu.VMEM((2, ROWS, depth), jnp.bfloat16),
            pltpu.SemaphoreType.DMA((len(chunks),)),
            pltpu.SemaphoreType.DMA((2,)),
        ],
        compiler_params=pltpu.CompilerParams(vmem_limit_bytes=40 * 2**20),
        cost_estimate=pl.CostEstimate(
            flops=int(2 * height * depth * columns * COST),
            bytes_accessed=int(2 * depth * (height + columns) * COST),
            transcendentals=0,
        ),
    )(*operands)


TILE = 1024
LANES = 128


def shared_kernel(in_steps, hidden, adapter_in, cotangent, adapter_out, out):
    number = pl.program_id(0)
    rank = adapter_in.shape[0]
    contract_last = (((1,), (1,)), ((), ()))

    @pl.when(number == 0)
    def _():
        out[...] = jnp.zeros_like(out)

    @pl.when(number < in_steps)
    def _():
        rows = hidden[...]
        out[:, :rank] += lax.dot_general(
            rows, adapter_in[...], contract_last, preferred_element_type=jnp.float32
        )
        wide = rows.astype(jnp.float32)
        squares = jnp.sum(wide * wide, axis=1, keepdims=True)
        out[:, 2 * rank :] += jnp.broadcast_to(squares, (rows.shape[0], LANES))

    @pl.when(number >= in_steps)
    def _():
        out[:, rank : 2 * rank] += adapter_scale * lax.dot_general(
            cotangent[...], adapter_out[...], contract_last, preferred_element_type=jnp.float32
        )


def shared_sums(hidden, adapter_in, cotangent, adapter_out):
    tokens, rank = hidden.shape[0], adapter_in.shape[0]
    in_steps, out_steps = hidden.shape[1] // TILE, cotangent.shape[1] // TILE
    early = lambda i: (0, jnp.minimum(i, in_steps - 1))
    late = lambda i: (0, jnp.maximum(i - in_steps, 0))
    return pl.pallas_call(
        functools.partial(shared_kernel, in_steps),
        grid=(in_steps + out_steps,),
        out_shape=jax.ShapeDtypeStruct((tokens, 2 * rank + LANES), jnp.float32),
        in_specs=[
            pl.BlockSpec((tokens, TILE), early),
            pl.BlockSpec((rank, TILE), early),
            pl.BlockSpec((tokens, TILE), late),
            pl.BlockSpec((rank, TILE), late),
        ],
        out_specs=pl.BlockSpec((tokens, 2 * rank + LANES), lambda i: (0, 0)),
        compiler_params=pltpu.CompilerParams(vmem_limit_bytes=32 * 2**20),
        cost_estimate=pl.CostEstimate(
            flops=int(2 * tokens * rank * TILE * (in_steps + out_steps) * COST),
            bytes_accessed=int(2 * TILE * (tokens + rank) * (in_steps + out_steps) * COST),
            transcendentals=0,
        ),
    )(hidden, adapter_in, cotangent, adapter_out)


def lift_of(radius):
    square = radius * radius
    series = 1.0 + square / 6.0 * (
        1.0 + square / 20.0 * (1.0 + square / 42.0 * (1.0 + square / 72.0))
    )
    large = (jnp.exp(radius) - jnp.exp(-radius)) * 0.5 / radius
    return jnp.where(radius < 1.0, series, large)


def gradient_kernel(
    in_steps, feature_count, own, other, order, hidden, cotangent, tangent_out, sent, kept, left_in, left_out
):
    number = pl.program_id(0)
    rank, half = order.shape[0], sent.shape[0]

    @pl.when(number == 0)
    def _():
        total = own[...] + other[...]
        raw, tangent_grad = total[:, :rank], total[:, rank : 2 * rank]
        square_sum = total[:, 2 * rank : 2 * rank + 1]
        level = jnp.sqrt(square_sum / feature_count + tiny_eps)
        lift_factor = lift_of(exp_rate * level)
        lorentz = lift_factor * raw
        norm_value = jnp.sqrt(jnp.sum(lorentz * lorentz, axis=1, keepdims=True) + tiny_eps)
        phi_value = inverse_sinh(norm_value) / norm_value
        tangent = (phi_value * lorentz).astype(jnp.bfloat16)
        inner_value = jnp.sum(lorentz * tangent_grad, axis=1, keepdims=True)
        coefficient = (1.0 / jnp.sqrt(1.0 + norm_value * norm_value) - phi_value) / (
            norm_value * norm_value
        )
        lorentz_grad = phi_value * tangent_grad + (coefficient * inner_value) * lorentz
        raw_grad = (lift_factor * lorentz_grad).astype(jnp.bfloat16)
        tangent_out[...] = tangent
        contract_last = (((1,), (1,)), ((), ()))
        for target, value in ((left_in, raw_grad), (left_out, tangent)):
            target[...] = lax.dot_general(
                order[...], value, contract_last, preferred_element_type=jnp.float32
            ).astype(jnp.bfloat16)

    @pl.when(number < in_steps)
    def _():
        total = jnp.dot(left_in[...], hidden[...], preferred_element_type=jnp.float32)
        sent[...] = total[:half]
        kept[...] = total[half:]

    @pl.when(number >= in_steps)
    def _():
        total = adapter_scale * jnp.dot(
            left_out[...], cotangent[...], preferred_element_type=jnp.float32
        )
        sent[...] = total[:half]
        kept[...] = total[half:]


def gradients(own, other, order, feature_count, hidden, cotangent):
    rank, tokens = order.shape[0], hidden.shape[0]
    in_steps, out_steps = hidden.shape[1] // TILE, cotangent.shape[1] // TILE
    steps = in_steps + out_steps
    shape = jax.ShapeDtypeStruct((rank // 2, steps * TILE), jnp.float32)
    part = pl.BlockSpec((rank // 2, TILE), lambda i: (0, i))
    return pl.pallas_call(
        functools.partial(gradient_kernel, in_steps, feature_count),
        grid=(steps,),
        out_shape=(jax.ShapeDtypeStruct((tokens, rank), jnp.bfloat16), shape, shape),
        in_specs=[
            pl.BlockSpec(own.shape, lambda i: (0, 0)),
            pl.BlockSpec(own.shape, lambda i: (0, 0)),
            pl.BlockSpec(order.shape, lambda i: (0, 0)),
            pl.BlockSpec((tokens, TILE), lambda i: (0, jnp.minimum(i, in_steps - 1))),
            pl.BlockSpec((tokens, TILE), lambda i: (0, jnp.maximum(i - in_steps, 0))),
        ],
        out_specs=(pl.BlockSpec((tokens, rank), lambda i: (0, 0)), part, part),
        scratch_shapes=[pltpu.VMEM((rank, tokens), jnp.bfloat16)] * 2,
        compiler_params=pltpu.CompilerParams(vmem_limit_bytes=32 * 2**20),
        cost_estimate=pl.CostEstimate(
            flops=int(2 * rank * tokens * steps * TILE * COST),
            bytes_accessed=int((2 * tokens + 4 * rank) * steps * TILE * COST),
            transcendentals=0,
        ),
    )(own, other, order, hidden, cotangent)


def assemble_kernel(code, *refs):
    out = refs[-1]
    for number, piece in enumerate(refs[:-1]):

        @pl.when(pl.program_id(0) == number)
        def _(piece=piece):
            out[...] = piece[...]


def assemble(places, pieces):
    tokens, columns = pieces[0].shape
    return pl.pallas_call(
        assemble_kernel,
        grid_spec=pltpu.PrefetchScalarGridSpec(
            num_scalar_prefetch=1,
            grid=(len(pieces),),
            in_specs=[pl.BlockSpec((tokens, columns), lambda i, code: (0, 0))] * len(pieces),
            out_specs=pl.BlockSpec((tokens, columns), lambda i, code: (0, code[i])),
        ),
        out_shape=jax.ShapeDtypeStruct((tokens, columns * len(pieces)), pieces[0].dtype),
        compiler_params=pltpu.CompilerParams(vmem_limit_bytes=32 * 2**20),
    )(jnp.stack(places).astype(jnp.int32), *pieces)


class Held(dict):
    def gate(self, *names):
        names = list(dict.fromkeys(names))
        for name, value in zip(names, lax.optimization_barrier(tuple(self[n] for n in names))):
            self[name] = value

    def all(self, letter, numbers):
        return [self[letter, i] for i in numbers]


def fast_shards(hidden, base_weight, adapter_in, adapter_out, cotangent):
    feature_count = hidden.shape[1] * 2
    tokens, depth = hidden.shape
    columns = base_weight.shape[1]
    place = lax.axis_index("dp")
    z, member = place // GROUP, place % GROUP
    x, core = member // 2, member % 2
    y = lax.axis_index("tensor")
    outer = jnp.logical_or(z == 0, z == LINE - 1)
    inner = jnp.logical_not(outer)
    early = (z // 2) == y
    late = jnp.logical_not(early)
    side = jnp.where(z < 2, 0, 1)
    scale = jnp.float32(adapter_scale)
    parts, slots = 4, 3 * HALVES
    rows, step = depth // HALVES, tokens // parts
    held = Held()
    held["own", 0], held["x", 0] = base_weight[:rows], hidden[:step]
    held["weight"], held["hidden"] = base_weight, hidden

    def send_weight(s):
        hop = s // HALVES
        if hop == LINE - 2:
            far = [jnp.where(side == 0, held["left", q], held["right", q]) for q in (2, 3)]
            far.append(held["own", 1])
            sent = jnp.where(jnp.logical_and(early, inner), far[s - 3], far[s - 4])
            pairs = line_pairs([1], -1) + line_pairs([LINE - 2], 1)
            held["left", s] = held["right", s] = lax.ppermute(sent, "dp", pairs)
            return
        for name, sign, last in (("left", -1, 1), ("right", 1, LINE - 2)):
            sent = held["own", s] if s < HALVES else held[name, s - HALVES]
            if s > 0:
                other = held[name, s - 1]
                sent = jnp.where(jnp.logical_and(early, z == last), other, sent)
            sources = [q for q in range(LINE) if 0 <= q + sign < LINE and 0 <= q - sign * hop < LINE]
            held[name, s] = lax.ppermute(sent, "dp", line_pairs(sources, sign))

    def send_hidden(i):
        held["x", i] = lax.ppermute(held["x", i], "dp", x_swap)
        if i + 1 < parts:
            held["x", i + 1] = held["hidden"][(i + 1) * step : (i + 2) * step]

    def over_core(name, result=None):
        held[result or name] = lax.ppermute(held[name], "dp", core_swap)

    def pass_hidden(i):
        over_core(("x", i), ("far", i))

    def send_sums(k):
        sent = lax.dynamic_index_in_dim(held["mine"], z ^ k, 0, False).astype(jnp.bfloat16)
        pairs = [(q * GROUP + r, (q ^ k) * GROUP + r) for q in range(LINE) for r in range(GROUP)]
        held["got", k] = lax.ppermute(sent, "dp", pairs)

    def codes(default, *cases):
        return pick(cases, default).astype(jnp.int32)[None]

    def streams(*numbers):
        return [(held[name, s], 0) for s in numbers for name in ("left", "right")]

    def window(s, *names):
        names = [("left", s), ("right", s), "weight", *names]
        held.gate(*names)
        held["own", 1] = held["weight"][rows:]
        if s < LINE - 1:
            send_weight(s + 1)
        if s == LINE - 1:
            send_weight(s + 1)
            send_weight(s + 2)

    end_early = jnp.logical_and(outer, early)
    end_late = jnp.logical_and(outer, late)
    inner_late = jnp.logical_and(inner, late)
    none = jnp.zeros((1,), jnp.int32)
    first_code = codes(2 + side, (end_early, side), (inner_late, 3 - side))
    first_code = jnp.concatenate([first_code] * HALVES)
    second_code = codes(4 + side, (end_early, side), (inner_late, 2 + side))
    second_code = jnp.concatenate([second_code] * HALVES)
    third_code = [
        codes(
            1 - side,
            (end_early, side + (0 if q == 0 else 2)),
            (end_late, 2 + side),
            (inner_late, 4 + side),
        )
        for q in range(HALVES)
    ]

    send_weight(0)
    send_hidden(0)
    held["core"] = lax.ppermute(hidden, "dp", core_swap)
    held["shared"] = shared_sums(hidden, adapter_in, cotangent, adapter_out)
    held["shared other"] = lax.ppermute(held["shared"], "tensor", pair_swap)
    rank = adapter_in.shape[0]
    share = rank // (LINE * GROUP)
    row = jnp.arange(rank)
    which = row // (LINE * share)
    owner = member ^ jnp.where(which == 0, 3, jnp.where(which == 1, 1, jnp.where(which == 2, 2, 0)))
    column = (row // share % LINE) * (GROUP * share) + owner * share + row % share
    held["order"] = (column[:, None] == jnp.arange(rank)[None, :]).astype(jnp.bfloat16)

    window(0, ("x", 0), ("x", 1), "hidden")
    send_hidden(1)
    held["t", 0], held["sent"], held["kept"] = gradients(
        held["shared"], held["shared other"], held["order"], feature_count, hidden, cotangent
    )
    over_core("sent")

    window(1, ("x", 1), ("x", 2), "hidden", "core", "kept", ("t", 0))
    send_hidden(2)
    pass_hidden(0)
    near = [hidden, held["core"]]
    whole_weight = [[(base_weight, 0)]]
    held["own sum", 0] = product(none, depth, whole_weight, near)

    window(2, ("x", 2), ("x", 3), ("far", 0), "sent", "kept", ("own sum", 0))
    send_hidden(3)
    pass_hidden(1)
    pass_hidden(2)
    sums = held["kept"] + held["sent"]
    flat = sums[: rank // 4].astype(jnp.bfloat16)
    held["sent"] = jnp.concatenate([flat, held["t", 0].reshape(flat.shape[0], -1)], axis=1)
    held["kept"] = sums[rank // 4 :]
    first = [streams(1 + q, q) for q in range(HALVES)]
    held["first sum", 0] = product(first_code, rows, first, near)

    held["y", 0] = jnp.where(early, held["first sum", 0], held["own sum", 0])

    window(3, ("x", 3), ("far", 1), ("far", 2), "sent", "kept", ("first sum", 0), ("y", 0))
    pass_hidden(3)
    held["sent"] = lax.ppermute(held["sent"], "dp", x_swap)
    held["y", 0] = lax.ppermute(held["y", 0], "tensor", pair_swap)
    half = parts // 2
    for h in (1, 2):
        pieces = range((h - 1) * half, h * half)
        members = held.all("x", pieces) + held.all("far", pieces)
        held["own sum", h] = product(none, depth, whole_weight, members)
        held["first sum", h] = product(first_code, rows, first, members)

    def in_order(name):
        a, b = held[name, 1], held[name, 2]
        cut = a.shape[0] // 2
        return jnp.concatenate([a[:cut], b[:cut], a[cut:], b[cut:]])

    first_sums = [held["first sum", 0], in_order("first sum")]
    own_sums = [held["own sum", 0], in_order("own sum")]
    held["y", 1] = lax.ppermute(
        jnp.where(early, first_sums[1], own_sums[1]), "tensor", pair_swap
    )

    far = held.all("x", range(parts)) + held.all("far", range(parts))
    groups = (near, far)
    second = [streams(3, 0, 2)]
    held["half code"] = second_code[:1]
    held.gate(("first sum", 1), ("first sum", 2), "half code")
    for h in range(2):
        held["half", h] = product(held["half code"], rows, second, groups[h])
    width = held["kept"].shape[1]
    held["t", 2] = held["sent"][:, width:].reshape(tokens, -1)
    held["mine"] = held["kept"] + held["sent"][:, :width].astype(jnp.float32)
    held["mine"] = held["mine"].reshape(LINE, share, -1)

    window(4, "mine", ("t", 2), ("far", 3), ("y", 0), ("y", 1), ("t", 0), ("half", 0), ("half", 1))
    for m in (0, 2):
        held["t", m + 1] = held["t", m]
        over_core(("t", m + 1))
    mixed = [streams(0, 4, 2), streams(4, 1, 3)]
    parity = (z % 2) ^ inner_late.astype(jnp.int32)
    blocks = [(parity ^ turn) * GROUP for turn in range(2)]
    factors = [
        lax.dynamic_slice_in_dim(adapter_out, (block + member) * columns, columns, 1)
        for block in blocks
    ]
    swaps = (None, core_swap, x_swap, both_swap)
    numbers = ((0, 1), (2, 3))
    places, pieces = [], []

    def give_out(turn, h, value):
        for i, m in reversed(list(enumerate(numbers[h]))):
            piece = value[i * tokens : (i + 1) * tokens]
            if m:
                piece = lax.ppermute(piece, "dp", swaps[m])
            places.append(blocks[turn] + (member ^ m))
            pieces.append(piece)

    group_tangents = [jnp.concatenate(held.all("t", numbers[h])) for h in range(2)]
    mixed_code = jnp.concatenate([third_code[0], second_code[1:], early.astype(jnp.int32)[None]])
    for h in (1, 0):
        extra = (
            held["half", h], first_sums[h], own_sums[h], held["y", h], group_tangents[h], factors[0]
        )
        held["w", h], held["total", h], held["third sum", h] = product(
            mixed_code, rows, mixed, groups[h], extra=extra, dtype=jnp.bfloat16
        )
        held["w", h] = lax.ppermute(held["w", h], "tensor", pair_swap)
        if h:
            held.gate(("third sum", h), "mine")
            for k in (1, 2, 3):
                send_sums(k)
    for h in (1, 0):
        give_out(0, h, held["total", h])

    window(5, ("third sum", 0), ("third sum", 1))
    for h in (1, 0):
        chunk = [streams(1, 5, 3)]
        extra = (held["third sum", h], held["w", h], group_tangents[h], factors[1])
        value = product(third_code[1], rows, chunk, groups[h], rows, extra, jnp.bfloat16)
        give_out(1, h, value)
    output = assemble(places, pieces)
    grads = lax.dynamic_index_in_dim(held["mine"], z, 0, False)
    held["grads"] = sum((held["got", k].astype(jnp.float32) for k in (1, 2, 3)), grads)
    return (output, held["grads"][:, :depth], held["grads"][:, depth:])


def solution(mesh):
    fits = mesh.shape["dp"] == LINE * GROUP and mesh.shape["tensor"] == 2
    return jax.shard_map(
        fast_shards if fits else plain_shards,
        mesh=mesh,
        in_specs=(
            P("dp", "tensor"),
            P("tensor", "dp"),
            P(None, "tensor"),
            P(None, "tensor"),
            P("dp", "tensor"),
        ),
        out_specs=(P("dp", "tensor"), P("dp", "tensor"), P("dp", "tensor")),
        check_vma=False,
    )
```

```python
import functools

import jax
import jax.numpy as jnp
from jax import lax
from jax.experimental import pallas as pl
from jax.experimental.pallas import tpu as pltpu
from jax.sharding import PartitionSpec as P

adapter_scale = 4.0
exp_rate = 0.25
tiny_eps = 1e-06


def inverse_sinh(value):
    return jnp.log(value + jnp.sqrt(1.0 + value * value))


def plain_shards(hidden, base_weight, adapter_in, adapter_out, cotangent):
    feature_count = hidden.shape[1] * lax.axis_size("tensor")
    contract_last = (((1,), (1,)), ((), ()))
    contract_first = (((0,), (0,)), ((), ()))
    square_part = jnp.sum(jnp.square(hidden.astype(jnp.float32)), axis=1)
    rank_part = lax.dot_general(
        hidden, adapter_in, contract_last, preferred_element_type=jnp.float32
    )
    square_sum, lorentz_raw = lax.psum((square_part, rank_part), "tensor")
    level = jnp.sqrt(square_sum / feature_count + tiny_eps)
    radius = exp_rate * level
    lift_factor = jnp.sinh(radius) / radius
    lorentz = lift_factor[:, None] * lorentz_raw
    norm_value = jnp.sqrt(jnp.sum(lorentz * lorentz, axis=1) + tiny_eps)
    phi_value = inverse_sinh(norm_value) / norm_value
    tangent = (phi_value[:, None] * lorentz).astype(jnp.bfloat16)
    partial_cols = jnp.dot(
        hidden,
        lax.all_gather(base_weight, "dp", axis=1, tiled=True),
        preferred_element_type=jnp.float32,
    )
    base_sum = lax.psum_scatter(partial_cols, "tensor", scatter_dimension=1, tiled=True)
    adapter_term = jnp.dot(tangent, adapter_out, preferred_element_type=jnp.float32)
    output = (base_sum + adapter_scale * adapter_term).astype(jnp.bfloat16)
    out_part = adapter_scale * lax.dot_general(
        tangent, cotangent, contract_first, preferred_element_type=jnp.float32
    )
    cotan_later = adapter_scale * lax.dot_general(
        cotangent, adapter_out, contract_last, preferred_element_type=jnp.float32
    )
    tangent_grad = lax.psum(cotan_later, "tensor")
    inner_value = jnp.sum(lorentz * tangent_grad, axis=1)
    coefficient = (1.0 / jnp.sqrt(1.0 + norm_value * norm_value) - phi_value) / (
        norm_value * norm_value
    )
    lorentz_grad = (
        phi_value[:, None] * tangent_grad + (coefficient * inner_value)[:, None] * lorentz
    )
    raw_grad = (lift_factor[:, None] * lorentz_grad).astype(jnp.bfloat16)
    in_part = lax.dot_general(raw_grad, hidden, contract_first, preferred_element_type=jnp.float32)
    grad_in, grad_out = (
        lax.psum_scatter(in_part, "dp", scatter_dimension=0, tiled=True),
        lax.psum_scatter(out_part, "dp", scatter_dimension=0, tiled=True),
    )
    return (output, grad_in, grad_out)


GROUP = 4
LINE = 4
HALVES = 2
core_swap = [(d, d ^ 1) for d in range(LINE * GROUP)]
x_swap = [(d, d ^ 2) for d in range(LINE * GROUP)]
both_swap = [(d, d ^ 3) for d in range(LINE * GROUP)]
pair_swap = [(0, 1), (1, 0)]


def line_pairs(sources, step):
    return [(z * GROUP + r, (z + step) * GROUP + r) for z in sources for r in range(GROUP)]


def pick(cases, default):
    out = default
    for condition, value in cases:
        out = jnp.where(condition, value, out)
    return out


def dot32(a, b):
    return jnp.dot(a, b, preferred_element_type=jnp.float32)


ROWS = 256
COST = 0.01


def product_kernel(plan, sources, blocks, has_base, *refs):
    code, refs = refs[0], refs[1:]
    weights, refs = refs[: sources[0]], refs[sources[0] :]
    hiddens, refs = refs[: sources[1]], refs[sources[1] :]
    extra, refs = refs[:has_base], refs[has_base:]
    outs, (weight, slots, weight_sem, slot_sems) = refs[:-4], refs[-4:]
    out = outs[0]
    first_column = plan[1]
    depth = weight.shape[0]
    step = depth // len(plan[0])

    def weight_copy(c, candidate):
        source, row = candidate
        return pltpu.make_async_copy(
            weights[source].at[pl.ds(row, step)],
            weight.at[pl.ds(c * step, step)],
            weight_sem.at[c],
        )

    def hidden_copies(b):
        copies, at = [], 0
        for source, row, rows in blocks[b]:
            copies.append(
                pltpu.make_async_copy(
                    hiddens[source].at[pl.ds(row, rows), pl.ds(first_column, depth)],
                    slots.at[b % 2, pl.ds(at, rows)],
                    slot_sems.at[b % 2],
                )
            )
            at += rows
        return copies

    for copy in hidden_copies(0):
        copy.start()
    for c, candidates in enumerate(plan[0]):
        if len(candidates) == 1:
            weight_copy(c, candidates[0]).start()
        for number, candidate in enumerate(candidates if len(candidates) > 1 else ()):

            @pl.when(code[c] == number)
            def _(c=c, candidate=candidate):
                weight_copy(c, candidate).start()

    for copy in hidden_copies(1):
        copy.start()
    for c, candidates in enumerate(plan[0]):
        weight_copy(c, candidates[0]).wait()

    def body(b, carry):
        slot = lax.rem(b, 2)
        for number in range(len(blocks)):

            @pl.when(b == number)
            def _(number=number):
                for copy in hidden_copies(number):
                    copy.wait()

        rows = pl.ds(pl.multiple_of(b * ROWS, ROWS), ROWS)
        if len(extra) == 6:
            third = jnp.dot(
                slots[slot, :, :step], weight[:step], preferred_element_type=jnp.float32
            )
            outs[2][rows, :] = third
            total = extra[0][rows, :] + jnp.dot(
                slots[slot, :, step:], weight[step:], preferred_element_type=jnp.float32
            )
        else:
            total = jnp.dot(slots[slot], weight[...], preferred_element_type=jnp.float32)
        if len(extra) > 0:
            other, tangent, factor = extra[-3:]
            term = jnp.dot(tangent[rows, :], factor[...], preferred_element_type=jnp.float32)
            term = other[rows, :].astype(jnp.float32) + jnp.float32(adapter_scale) * term
        if len(extra) == 6:
            gives = code[len(plan[0])] == 1
            first, own = extra[1][rows, :], extra[2][rows, :]
            outs[1][rows, :] = (jnp.where(gives, own, total) + term).astype(outs[1].dtype)
            total = jnp.where(gives, total, first)
        elif len(extra) == 4:
            total = total + extra[0][rows, :] + term
        out[rows, :] = total.astype(out.dtype)
        for number in range(2, len(blocks)):

            @pl.when(b + 2 == number)
            def _(number=number):
                for copy in hidden_copies(number):
                    copy.start()

        return carry

    lax.fori_loop(0, len(blocks), body, 0)


def product(code, step, chunks, hiddens, first_column=0, extra=(), dtype=jnp.float32):
    weights, candidates = [], []
    for chunk in chunks:
        for array, _ in chunk:
            if not any(array is weight for weight in weights):
                weights.append(array)
        candidates.append(
            tuple(
                ([array is weight for weight in weights].index(True), row) for array, row in chunk
            )
        )
    depth = step * len(chunks)
    columns = weights[0].shape[1]
    blocks, room = [], 0
    for number, array in enumerate(hiddens):
        row = 0
        while row < array.shape[0]:
            if room == 0:
                blocks.append([])
                room = ROWS
            rows = min(room, array.shape[0] - row)
            blocks[-1].append((number, row, rows))
            row, room = row + rows, room - rows
    height = len(blocks) * ROWS
    anywhere = pl.BlockSpec(memory_space=pl.ANY)
    whole = pl.BlockSpec(memory_space=pltpu.VMEM)
    operands = [code, *weights, *hiddens, *extra]
    in_specs = [pl.BlockSpec(memory_space=pltpu.SMEM)]
    in_specs += [anywhere] * (len(weights) + len(hiddens)) + [whole] * len(extra)
    kernel = functools.partial(
        product_kernel,
        (tuple(candidates), first_column),
        (len(weights), len(hiddens)),
        blocks,
        len(extra),
    )
    shape = jax.ShapeDtypeStruct((height, columns), dtype)
    shapes = (shape, shape, jax.ShapeDtypeStruct((height, columns), jnp.float32))
    several = len(extra) == 6
    return pl.pallas_call(
        kernel,
        out_shape=shapes if several else shape,
        in_specs=in_specs,
        out_specs=(whole,) * 3 if several else whole,
        scratch_shapes=[
            pltpu.VMEM((depth, columns), jnp.bfloat16),
            pltpu.VMEM((2, ROWS, depth), jnp.bfloat16),
            pltpu.SemaphoreType.DMA((len(chunks),)),
            pltpu.SemaphoreType.DMA((2,)),
        ],
        compiler_params=pltpu.CompilerParams(vmem_limit_bytes=40 * 2**20),
        cost_estimate=pl.CostEstimate(
            flops=int(2 * height * depth * columns * COST),
            bytes_accessed=int(2 * depth * (height + columns) * COST),
            transcendentals=0,
        ),
    )(*operands)


TILE = 1024
LANES = 128


def shared_kernel(in_steps, hidden, adapter_in, cotangent, adapter_out, out):
    number = pl.program_id(0)
    rank = adapter_in.shape[0]
    contract_last = (((1,), (1,)), ((), ()))

    @pl.when(number == 0)
    def _():
        out[...] = jnp.zeros_like(out)

    @pl.when(number < in_steps)
    def _():
        rows = hidden[...]
        out[:, :rank] += lax.dot_general(
            rows, adapter_in[...], contract_last, preferred_element_type=jnp.float32
        )
        wide = rows.astype(jnp.float32)
        squares = jnp.sum(wide * wide, axis=1, keepdims=True)
        out[:, 2 * rank :] += jnp.broadcast_to(squares, (rows.shape[0], LANES))

    @pl.when(number >= in_steps)
    def _():
        out[:, rank : 2 * rank] += adapter_scale * lax.dot_general(
            cotangent[...], adapter_out[...], contract_last, preferred_element_type=jnp.float32
        )


def shared_sums(hidden, adapter_in, cotangent, adapter_out):
    tokens, rank = hidden.shape[0], adapter_in.shape[0]
    in_steps, out_steps = hidden.shape[1] // TILE, cotangent.shape[1] // TILE
    early = lambda i: (0, jnp.minimum(i, in_steps - 1))
    late = lambda i: (0, jnp.maximum(i - in_steps, 0))
    return pl.pallas_call(
        functools.partial(shared_kernel, in_steps),
        grid=(in_steps + out_steps,),
        out_shape=jax.ShapeDtypeStruct((tokens, 2 * rank + LANES), jnp.float32),
        in_specs=[
            pl.BlockSpec((tokens, TILE), early),
            pl.BlockSpec((rank, TILE), early),
            pl.BlockSpec((tokens, TILE), late),
            pl.BlockSpec((rank, TILE), late),
        ],
        out_specs=pl.BlockSpec((tokens, 2 * rank + LANES), lambda i: (0, 0)),
        compiler_params=pltpu.CompilerParams(vmem_limit_bytes=32 * 2**20),
        cost_estimate=pl.CostEstimate(
            flops=int(2 * tokens * rank * TILE * (in_steps + out_steps) * COST),
            bytes_accessed=int(2 * TILE * (tokens + rank) * (in_steps + out_steps) * COST),
            transcendentals=0,
        ),
    )(hidden, adapter_in, cotangent, adapter_out)


def lift_of(radius):
    square = radius * radius
    series = 1.0 + square / 6.0 * (
        1.0 + square / 20.0 * (1.0 + square / 42.0 * (1.0 + square / 72.0))
    )
    large = (jnp.exp(radius) - jnp.exp(-radius)) * 0.5 / radius
    return jnp.where(radius < 1.0, series, large)


def gradient_kernel(
    in_steps, feature_count, own, other, order, hidden, cotangent, tangent_out, sent, kept, left_in, left_out
):
    number = pl.program_id(0)
    rank, half = order.shape[0], sent.shape[0]

    @pl.when(number == 0)
    def _():
        total = own[...] + other[...]
        raw, tangent_grad = total[:, :rank], total[:, rank : 2 * rank]
        square_sum = total[:, 2 * rank : 2 * rank + 1]
        level = jnp.sqrt(square_sum / feature_count + tiny_eps)
        lift_factor = lift_of(exp_rate * level)
        lorentz = lift_factor * raw
        norm_value = jnp.sqrt(jnp.sum(lorentz * lorentz, axis=1, keepdims=True) + tiny_eps)
        phi_value = inverse_sinh(norm_value) / norm_value
        tangent = (phi_value * lorentz).astype(jnp.bfloat16)
        inner_value = jnp.sum(lorentz * tangent_grad, axis=1, keepdims=True)
        coefficient = (1.0 / jnp.sqrt(1.0 + norm_value * norm_value) - phi_value) / (
            norm_value * norm_value
        )
        lorentz_grad = phi_value * tangent_grad + (coefficient * inner_value) * lorentz
        raw_grad = (lift_factor * lorentz_grad).astype(jnp.bfloat16)
        tangent_out[...] = tangent
        contract_last = (((1,), (1,)), ((), ()))
        for target, value in ((left_in, raw_grad), (left_out, tangent)):
            target[...] = lax.dot_general(
                order[...], value, contract_last, preferred_element_type=jnp.float32
            ).astype(jnp.bfloat16)

    @pl.when(number < in_steps)
    def _():
        total = jnp.dot(left_in[...], hidden[...], preferred_element_type=jnp.float32)
        sent[...] = total[:half]
        kept[...] = total[half:]

    @pl.when(number >= in_steps)
    def _():
        total = adapter_scale * jnp.dot(
            left_out[...], cotangent[...], preferred_element_type=jnp.float32
        )
        sent[...] = total[:half]
        kept[...] = total[half:]


def gradients(own, other, order, feature_count, hidden, cotangent):
    rank, tokens = order.shape[0], hidden.shape[0]
    in_steps, out_steps = hidden.shape[1] // TILE, cotangent.shape[1] // TILE
    steps = in_steps + out_steps
    shape = jax.ShapeDtypeStruct((rank // 2, steps * TILE), jnp.float32)
    part = pl.BlockSpec((rank // 2, TILE), lambda i: (0, i))
    return pl.pallas_call(
        functools.partial(gradient_kernel, in_steps, feature_count),
        grid=(steps,),
        out_shape=(jax.ShapeDtypeStruct((tokens, rank), jnp.bfloat16), shape, shape),
        in_specs=[
            pl.BlockSpec(own.shape, lambda i: (0, 0)),
            pl.BlockSpec(own.shape, lambda i: (0, 0)),
            pl.BlockSpec(order.shape, lambda i: (0, 0)),
            pl.BlockSpec((tokens, TILE), lambda i: (0, jnp.minimum(i, in_steps - 1))),
            pl.BlockSpec((tokens, TILE), lambda i: (0, jnp.maximum(i - in_steps, 0))),
        ],
        out_specs=(pl.BlockSpec((tokens, rank), lambda i: (0, 0)), part, part),
        scratch_shapes=[pltpu.VMEM((rank, tokens), jnp.bfloat16)] * 2,
        compiler_params=pltpu.CompilerParams(vmem_limit_bytes=32 * 2**20),
        cost_estimate=pl.CostEstimate(
            flops=int(2 * rank * tokens * steps * TILE * COST),
            bytes_accessed=int((2 * tokens + 4 * rank) * steps * TILE * COST),
            transcendentals=0,
        ),
    )(own, other, order, hidden, cotangent)


def assemble_kernel(code, *refs):
    out = refs[-1]
    for number, piece in enumerate(refs[:-1]):

        @pl.when(pl.program_id(0) == number)
        def _(piece=piece):
            out[...] = piece[...]


def assemble(places, pieces):
    tokens, columns = pieces[0].shape
    return pl.pallas_call(
        assemble_kernel,
        grid_spec=pltpu.PrefetchScalarGridSpec(
            num_scalar_prefetch=1,
            grid=(len(pieces),),
            in_specs=[pl.BlockSpec((tokens, columns), lambda i, code: (0, 0))] * len(pieces),
            out_specs=pl.BlockSpec((tokens, columns), lambda i, code: (0, code[i])),
        ),
        out_shape=jax.ShapeDtypeStruct((tokens, columns * len(pieces)), pieces[0].dtype),
        compiler_params=pltpu.CompilerParams(vmem_limit_bytes=32 * 2**20),
    )(jnp.stack(places).astype(jnp.int32), *pieces)


class Held(dict):
    def gate(self, *names):
        names = list(dict.fromkeys(names))
        for name, value in zip(names, lax.optimization_barrier(tuple(self[n] for n in names))):
            self[name] = value

    def all(self, letter, numbers):
        return [self[letter, i] for i in numbers]


def fast_shards(hidden, base_weight, adapter_in, adapter_out, cotangent):
    feature_count = hidden.shape[1] * 2
    tokens, depth = hidden.shape
    columns = base_weight.shape[1]
    place = lax.axis_index("dp")
    z, member = place // GROUP, place % GROUP
    x, core = member // 2, member % 2
    y = lax.axis_index("tensor")
    outer = jnp.logical_or(z == 0, z == LINE - 1)
    inner = jnp.logical_not(outer)
    early = (z // 2) == y
    late = jnp.logical_not(early)
    side = jnp.where(z < 2, 0, 1)
    scale = jnp.float32(adapter_scale)
    parts, slots = 4, 3 * HALVES
    rows, step = depth // HALVES, tokens // parts
    held = Held()
    held["own", 0], held["x", 0] = base_weight[:rows], hidden[:step]
    held["weight"], held["hidden"] = base_weight, hidden

    def send_weight(s):
        hop = s // HALVES
        if hop == LINE - 2:
            far = [jnp.where(side == 0, held["left", q], held["right", q]) for q in (2, 3)]
            far.append(held["own", 1])
            sent = jnp.where(jnp.logical_and(early, inner), far[s - 3], far[s - 4])
            pairs = line_pairs([1], -1) + line_pairs([LINE - 2], 1)
            held["left", s] = held["right", s] = lax.ppermute(sent, "dp", pairs)
            return
        for name, sign, last in (("left", -1, 1), ("right", 1, LINE - 2)):
            sent = held["own", s] if s < HALVES else held[name, s - HALVES]
            if s > 0:
                other = held[name, s - 1]
                sent = jnp.where(jnp.logical_and(early, z == last), other, sent)
            sources = [q for q in range(LINE) if 0 <= q + sign < LINE and 0 <= q - sign * hop < LINE]
            held[name, s] = lax.ppermute(sent, "dp", line_pairs(sources, sign))

    def send_hidden(i):
        held["x", i] = lax.ppermute(held["x", i], "dp", x_swap)
        if i + 1 < parts:
            held["x", i + 1] = held["hidden"][(i + 1) * step : (i + 2) * step]

    def over_core(name, result=None):
        held[result or name] = lax.ppermute(held[name], "dp", core_swap)

    def pass_hidden(i):
        over_core(("x", i), ("far", i))

    def send_sums(k):
        sent = lax.dynamic_index_in_dim(held["mine"], z ^ k, 0, False).astype(jnp.bfloat16)
        pairs = [(q * GROUP + r, (q ^ k) * GROUP + r) for q in range(LINE) for r in range(GROUP)]
        held["got", k] = lax.ppermute(sent, "dp", pairs)

    def codes(default, *cases):
        return pick(cases, default).astype(jnp.int32)[None]

    def streams(*numbers):
        return [(held[name, s], 0) for s in numbers for name in ("left", "right")]

    def window(s, *names):
        names = [("left", s), ("right", s), "weight", *names]
        held.gate(*names)
        held["own", 1] = held["weight"][rows:]
        if s < LINE - 1:
            send_weight(s + 1)
        if s == LINE - 1:
            send_weight(s + 1)
            send_weight(s + 2)

    end_early = jnp.logical_and(outer, early)
    end_late = jnp.logical_and(outer, late)
    inner_late = jnp.logical_and(inner, late)
    none = jnp.zeros((1,), jnp.int32)
    first_code = codes(2 + side, (end_early, side), (inner_late, 3 - side))
    first_code = jnp.concatenate([first_code] * HALVES)
    second_code = codes(4 + side, (end_early, side), (inner_late, 2 + side))
    second_code = jnp.concatenate([second_code] * HALVES)
    third_code = [
        codes(
            1 - side,
            (end_early, side + (0 if q == 0 else 2)),
            (end_late, 2 + side),
            (inner_late, 4 + side),
        )
        for q in range(HALVES)
    ]

    send_weight(0)
    send_hidden(0)
    held["core"] = lax.ppermute(hidden, "dp", core_swap)
    held["shared"] = shared_sums(hidden, adapter_in, cotangent, adapter_out)
    held["shared other"] = lax.ppermute(held["shared"], "tensor", pair_swap)
    rank = adapter_in.shape[0]
    share = rank // (LINE * GROUP)
    row = jnp.arange(rank)
    which = row // (LINE * share)
    owner = member ^ jnp.where(which == 0, 3, jnp.where(which == 1, 1, jnp.where(which == 2, 2, 0)))
    column = (row // share % LINE) * (GROUP * share) + owner * share + row % share
    held["order"] = (column[:, None] == jnp.arange(rank)[None, :]).astype(jnp.bfloat16)

    window(0, ("x", 0), ("x", 1), "hidden")
    send_hidden(1)
    held["t", 0], held["sent"], held["kept"] = gradients(
        held["shared"], held["shared other"], held["order"], feature_count, hidden, cotangent
    )
    over_core("sent")

    window(1, ("x", 1), ("x", 2), "hidden", "core", "kept", ("t", 0))
    send_hidden(2)
    pass_hidden(0)
    near = [hidden, held["core"]]
    whole_weight = [[(base_weight, 0)]]
    held["own sum", 0] = product(none, depth, whole_weight, near)

    window(2, ("x", 2), ("x", 3), ("far", 0), "sent", "kept", ("own sum", 0))
    send_hidden(3)
    pass_hidden(1)
    pass_hidden(2)
    sums = held["kept"] + held["sent"]
    flat = sums[: rank // 4].astype(jnp.bfloat16)
    held["sent"] = jnp.concatenate([flat, held["t", 0].reshape(flat.shape[0], -1)], axis=1)
    held["kept"] = sums[rank // 4 :]
    first = [streams(1 + q, q) for q in range(HALVES)]
    held["first sum", 0] = product(first_code, rows, first, near)

    held["y", 0] = jnp.where(early, held["first sum", 0], held["own sum", 0])

    window(3, ("x", 3), ("far", 1), ("far", 2), "sent", "kept", ("first sum", 0), ("y", 0))
    pass_hidden(3)
    held["sent"] = lax.ppermute(held["sent"], "dp", x_swap)
    held["y", 0] = lax.ppermute(held["y", 0], "tensor", pair_swap)
    half = parts // 2
    for h in (1, 2):
        pieces = range((h - 1) * half, h * half)
        members = held.all("x", pieces) + held.all("far", pieces)
        held["own sum", h] = product(none, depth, whole_weight, members)
        held["first sum", h] = product(first_code, rows, first, members)

    def in_order(name):
        a, b = held[name, 1], held[name, 2]
        cut = a.shape[0] // 2
        return jnp.concatenate([a[:cut], b[:cut], a[cut:], b[cut:]])

    first_sums = [held["first sum", 0], in_order("first sum")]
    own_sums = [held["own sum", 0], in_order("own sum")]
    held["y", 1] = lax.ppermute(
        jnp.where(early, first_sums[1], own_sums[1]), "tensor", pair_swap
    )

    far = held.all("x", range(parts)) + held.all("far", range(parts))
    groups = (near, far)
    second = [streams(3, 0, 2)]
    held["half code"] = second_code[:1]
    held.gate(("first sum", 1), ("first sum", 2), "half code")
    for h in range(2):
        held["half", h] = product(held["half code"], rows, second, groups[h])
    width = held["kept"].shape[1]
    held["t", 2] = held["sent"][:, width:].reshape(tokens, -1)
    held["mine"] = held["kept"] + held["sent"][:, :width].astype(jnp.float32)
    held["mine"] = held["mine"].reshape(LINE, share, -1)

    window(4, "mine", ("t", 2), ("far", 3), ("y", 0), ("y", 1), ("t", 0), ("half", 0), ("half", 1))
    for m in (0, 2):
        held["t", m + 1] = held["t", m]
        over_core(("t", m + 1))
    mixed = [streams(0, 4, 2), streams(4, 1, 3)]
    parity = (z % 2) ^ inner_late.astype(jnp.int32)
    blocks = [(parity ^ turn) * GROUP for turn in range(2)]
    factors = [
        lax.dynamic_slice_in_dim(adapter_out, (block + member) * columns, columns, 1)
        for block in blocks
    ]
    swaps = (None, core_swap, x_swap, both_swap)
    numbers = ((0, 1), (2, 3))
    places, pieces = [], []

    def give_out(turn, h, value):
        for i, m in reversed(list(enumerate(numbers[h]))):
            piece = value[i * tokens : (i + 1) * tokens]
            if m:
                piece = lax.ppermute(piece, "dp", swaps[m])
            places.append(blocks[turn] + (member ^ m))
            pieces.append(piece)

    group_tangents = [jnp.concatenate(held.all("t", numbers[h])) for h in range(2)]
    mixed_code = jnp.concatenate([third_code[0], second_code[1:], early.astype(jnp.int32)[None]])
    for h in (1, 0):
        extra = (
            held["half", h], first_sums[h], own_sums[h], held["y", h], group_tangents[h], factors[0]
        )
        held["w", h], held["total", h], held["third sum", h] = product(
            mixed_code, rows, mixed, groups[h], extra=extra, dtype=jnp.bfloat16
        )
        held["w", h] = lax.ppermute(held["w", h], "tensor", pair_swap)
        if h:
            held.gate(("third sum", h), "mine")
            for k in (3, 2, 1):
                send_sums(k)
    for h in (1, 0):
        give_out(0, h, held["total", h])

    window(5, ("third sum", 0), ("third sum", 1))
    for h in (1, 0):
        chunk = [streams(1, 5, 3)]
        extra = (held["third sum", h], held["w", h], group_tangents[h], factors[1])
        value = product(third_code[1], rows, chunk, groups[h], rows, extra, jnp.bfloat16)
        give_out(1, h, value)
    output = assemble(places, pieces)
    grads = lax.dynamic_index_in_dim(held["mine"], z, 0, False)
    held["grads"] = sum((held["got", k].astype(jnp.float32) for k in (1, 2, 3)), grads)
    return (output, held["grads"][:, :depth], held["grads"][:, depth:])


def solution(mesh):
    fits = mesh.shape["dp"] == LINE * GROUP and mesh.shape["tensor"] == 2
    return jax.shard_map(
        fast_shards if fits else plain_shards,
        mesh=mesh,
        in_specs=(
            P("dp", "tensor"),
            P("tensor", "dp"),
            P(None, "tensor"),
            P(None, "tensor"),
            P("dp", "tensor"),
        ),
        out_specs=(P("dp", "tensor"), P("dp", "tensor"), P("dp", "tensor")),
        check_vma=False,
    )
```
